128 devices in a mesh: dp: 32 (over z, x, core), proto: 4 (over y).
Axes of the slice: x: 4, y: 4, z: 4, core: 2. Of those that a mesh axis runs over, the one named last changes fastest.
Arguments:
- teacher_feats: bfloat16 [8192, 256], P('dp'), may hold values from -10 to 10
- teacher_protos: bfloat16 [256, 65536], P(None, 'proto'), may hold values from -1 to 1
- student_feats: bfloat16 [8192, 256], P('dp'), may hold values from -10 to 10
- student_protos: bfloat16 [256, 65536], P(None, 'proto'), may hold values from -1 to 1
Outputs:
- grad_protos: float32 [256, 65536], P('dp', 'proto')
- grad_feats: float32 [8192, 256], P('dp')
The draws below stay inside these ranges and needn't reach their ends.
All inputs are finite; a program needn't handle non-finite values.
Results may differ from the reference program's by a relative error of at most 0.0028.
Values may be sent and summed in bfloat16 or wider, within the bound.
A program may use at most 192 MiB of HBM per device.

```python
import math
import jax
import jax.numpy as jnp
from jax import lax

D = 256
PROTOS = 65536
ITERS = 3
IMAGES = 8192


def rising(count, top):
    return 1.0 + (top - 1.0) * jnp.arange(count, dtype=jnp.float32) / count


def teacher_table(key):
    protos_table = jax.random.normal(jax.random.fold_in(key, 101), (D, PROTOS), jnp.float32) * D ** (-0.5)
    return jnp.clip(protos_table, -1.0, 1.0)


def student_table(key, top):
    protos_table = jax.random.normal(jax.random.fold_in(key, 201), (D, PROTOS), jnp.float32) * D ** (-0.5)
    protos_table = protos_table * rising(PROTOS, top)[None, :]
    return jnp.clip(protos_table, -1.0, 1.0)


def draw_teacher_protos(key, part):
    protos_table = teacher_table(key)
    return protos_table.astype(jnp.bfloat16)


def draw_teacher_feats(key, part):
    key = jax.random.fold_in(key, 3)
    base_rows = jax.random.normal(key, (IMAGES, D), jnp.float32) * D ** (-0.5)
    base_rows = base_rows * rising(IMAGES, 3.0)[:, None]
    return jnp.clip(base_rows, -10.0, 10.0).astype(jnp.bfloat16)


def draw_student_protos(key, part):
    protos_table = student_table(key, 3.0)
    return protos_table.astype(jnp.bfloat16)


def draw_student_feats(key, part):
    key = jax.random.fold_in(key, 5)
    base_rows = jax.random.normal(key, (IMAGES, D), jnp.float32) * D ** (-0.5)
    return jnp.clip(base_rows, -10.0, 10.0).astype(jnp.bfloat16)


def setup_inputs(seed: int = 0) -> dict:
    arg_keys = jax.random.split(jax.random.key(seed), 5)
    teacher_feats = draw_teacher_feats(jax.random.fold_in(arg_keys[4], 71), 0)
    teacher_protos = draw_teacher_protos(jax.random.fold_in(arg_keys[4], 71), 0)
    student_feats = draw_student_feats(jax.random.fold_in(arg_keys[4], 71), 0)
    student_protos = draw_student_protos(jax.random.fold_in(arg_keys[4], 71), 0)
    return {"teacher_feats": teacher_feats, "teacher_protos": teacher_protos, "student_feats": student_feats, "student_protos": student_protos}


TEACHER_TEMP = 0.04
STUDENT_TEMP = 0.1

def reference(teacher_feats, teacher_protos, student_feats, student_protos):
    block_rows = math.gcd(IMAGES, 512)
    block_count = IMAGES // block_rows
    teacher_blocks = teacher_feats.reshape(block_count, block_rows, D)

    def teacher_scores(features):
        return jnp.dot(features, teacher_protos, preferred_element_type=jnp.float32) / TEACHER_TEMP
    col_max = lax.optimization_barrier(jnp.max(lax.map(lambda features: lax.optimization_barrier(jnp.max(teacher_scores(features), axis=0)), teacher_blocks), axis=0))
    exp_table = lax.map(lambda features: jnp.exp(teacher_scores(features) - col_max[None, :]), teacher_blocks)
    exp_table = exp_table.reshape(IMAGES, PROTOS)
    row_scale = jnp.ones((IMAGES,), jnp.float32)
    col_scale = jnp.ones((PROTOS,), jnp.float32)
    for iteration in range(ITERS):
        col_scale = 1.0 / lax.optimization_barrier(jnp.sum(exp_table * row_scale[:, None], axis=0))
        row_scale = 1.0 / lax.optimization_barrier(jnp.sum(exp_table * col_scale[None, :], axis=1))
    inputs_block = (student_feats.reshape(block_count, block_rows, D), exp_table.reshape(block_count, block_rows, PROTOS), row_scale.reshape(block_count, block_rows))

    def student_block(head_total, pieces):
        features, exp_rows, scale_rows = pieces
        scores = jnp.dot(features, student_protos, preferred_element_type=jnp.float32) / STUDENT_TEMP
        row_top = lax.optimization_barrier(jnp.max(scores, axis=1, keepdims=True))
        shifted = jnp.exp(scores - row_top)
        probabilities = shifted / lax.optimization_barrier(jnp.sum(shifted, axis=1, keepdims=True))
        targets = exp_rows * col_scale[None, :] * scale_rows[:, None]
        grad_logits = ((probabilities - targets) * (PROTOS / STUDENT_TEMP)).astype(jnp.bfloat16)
        grad_rows = lax.dot_general(grad_logits, student_protos, (((1,), (1,)), ((), ())), preferred_element_type=jnp.float32) / math.sqrt(PROTOS)
        head_total = head_total + lax.dot_general(features, grad_logits, (((0,), (0,)), ((), ())), preferred_element_type=jnp.float32)
        return (head_total, grad_rows)
    head_total, grad_rows = lax.scan(student_block, jnp.zeros((D, PROTOS), jnp.float32), inputs_block)
    return (head_total / math.sqrt(IMAGES), grad_rows.reshape(IMAGES, D))
```

```python
import functools
import math

import jax
import jax.numpy as jnp
from jax import lax
from jax.experimental import pallas as pl
from jax.experimental.pallas import tpu as pltpu
from jax.sharding import PartitionSpec as P

MESH = pl.DeviceIdType.MESH
F32 = jnp.float32
BF16 = jnp.bfloat16

TEACHER_TEMP = 0.04
STUDENT_TEMP = 0.1
LOG2E = math.log2(math.e)
T_EXP = LOG2E / TEACHER_TEMP
S_EXP = LOG2E / STUDENT_TEMP

NX, NY, NZ, NC = 4, 4, 4, 2
BLK = 256
ROWS = NX * BLK
COLS = 4096
CH = 512
NCH = COLS // CH
D = 256
ITERS = 3


def kernel(
    tf_hbm, tp_hbm, sf_hbm, sp_hbm, outp, outf,
    E, S, G, Tp, Sp, SpT, Tf, Sf, SfT, racc, rbc, gbc, smx, sfac,
    mb, sb, cvec, col1, col1_in, col2, col2_in, rowp, row_in, stat, stat_in,
    gp, gp_in, zs, zs_in, xs, gfs, gfs_in, gfown,
    local_sem, t_send, t_recv, s_send, s_recv, c1_send, c1_recv, c_send, c_recv,
    r_send, r_recv, st_send, st_recv, gp_send, gp_recv, z_send, z_recv, x_send, x_recv,
    f_send, f_recv, y_send, y_recv,
):
    dp = lax.axis_index("dp")
    y = lax.axis_index("proto")
    z, x, c = dp // 8, (dp // 2) % 4, dp % 2

    def dev(dz, dx, dc, dy):
        zz, xx, cc, yy = (z + dz) % NZ, (x + dx) % NX, (c + dc) % NC, (y + dy) % NY
        return {"dp": zz * 8 + xx * 2 + cc, "proto": yy}

    xy = [(a, b) for a in range(NX) for b in range(NY) if (a, b) != (0, 0)]
    zc = [(a, b) for a in range(NZ) for b in range(NC) if (a, b) != (0, 0)]

    def send(src, dst, ssem, rsem, where):
        pltpu.make_async_remote_copy(
            src_ref=src, dst_ref=dst, send_sem=ssem, recv_sem=rsem, device_id=where, device_id_type=MESH
        ).start()

    def take(ref, sem):
        pltpu.make_async_copy(ref, ref, sem).wait()

    barrier = pltpu.get_barrier_semaphore()
    for a, b in xy:
        pl.semaphore_signal(barrier, inc=1, device_id=dev(0, a, 0, b), device_id_type=MESH)
    for a, b in zc:
        pl.semaphore_signal(barrier, inc=1, device_id=dev(a, 0, b, 0), device_id_type=MESH)

    mine = pl.ds(pl.multiple_of(x * COLS, COLS), COLS)
    loads = [
        pltpu.make_async_copy(tf_hbm, Tf.at[x], local_sem.at[0]),
        pltpu.make_async_copy(sf_hbm, Sf.at[x], local_sem.at[1]),
        pltpu.make_async_copy(tp_hbm.at[:, mine], Tp, local_sem.at[2]),
        pltpu.make_async_copy(sp_hbm.at[:, mine], Sp, local_sem.at[3]),
    ]
    for load in loads:
        load.start()
    loads[0].wait()
    loads[1].wait()
    pl.semaphore_wait(barrier, len(xy) + len(zc))
    for a in (1, 3, 2):
        send(Tf.at[x], Tf.at[x], t_send, t_recv.at[x], dev(0, a, 0, 0))
    for a in (1, 3, 2):
        send(Sf.at[x], Sf.at[x], s_send, s_recv.at[x], dev(0, a, 0, 0))

    def chunk(j):
        return pl.ds(pl.multiple_of(j * CH, CH), CH)

    def rows_at(i, n):
        return pl.ds(pl.multiple_of(i * n, n), n)

    def teacher_block(a):
        def body(j, _):
            s = jnp.dot(Tf[a], Tp[:, chunk(j)], preferred_element_type=F32)
            m = jnp.max(s, axis=0, keepdims=True)
            e = jnp.exp2((s - m) * T_EXP)
            E[rows_at(a, BLK), chunk(j)] = e
            mb[a, pl.ds(j, 1), :] = m
            sb[a, pl.ds(j, 1), :] = jnp.sum(e, axis=0, keepdims=True)
            return 0
        lax.fori_loop(0, NCH, body, 0)

    def lane_parts(v, op):
        out = v[:, :128]
        for q in range(1, v.shape[1] // 128):
            out = op(out, v[:, q * 128:(q + 1) * 128])
        return out

    def to_lanes(src, dst, op):
        for i in range(8):
            t = src[i * 128:(i + 1) * 128, :].T
            dst[i:i + 1, :] = op(t, axis=0, keepdims=True)

    def to_rows(v, dst):
        for i in range(8):
            dst[i * 128:(i + 1) * 128, :] = jnp.broadcast_to(v[i:i + 1, :], (128, 128)).T

    def student_block(a):
        base = a * BLK
        block = rows_at(a, BLK)

        def scores(j, _):
            s = jnp.dot(Sf[a], Sp[:, chunk(j)], preferred_element_type=F32)
            S[block, chunk(j)] = s
            m = lane_parts(s, jnp.maximum)

            @pl.when(j == 0)
            def _():
                smx[block, :] = m

            @pl.when(j > 0)
            def _():
                smx[block, :] = jnp.maximum(smx[block, :], m)
            return 0
        lax.fori_loop(0, NCH, scores, 0)

        def exps(i, _):
            r = pl.ds(pl.multiple_of(base + i * 64, 64), 64)
            m = jnp.broadcast_to(jnp.max(smx[r, :], axis=1, keepdims=True), (64, 128))
            smx[r, :] = m
            acc = jnp.zeros((64, 128), F32)
            for q in range(COLS // 128):
                e = jnp.exp2((S[r, q * 128:(q + 1) * 128] - m) * S_EXP)
                S[r, q * 128:(q + 1) * 128] = e
                acc = acc + e
            sfac[r, :] = acc
            return 0
        lax.fori_loop(0, BLK // 64, exps, 0)

    def row_pass(first, last):
        def body(i, _):
            r = rows_at(i, 64)
            acc = jnp.zeros((64, 128), F32)
            for j in range(NCH):
                for q in range(CH // 128):
                    at = j * CH + q * 128
                    e = E[r, at:at + 128]
                    if first:
                        e = e * col1[0, j:j + 1, q * 128:(q + 1) * 128]
                        E[r, at:at + 128] = e
                    e = e * cvec[j:j + 1, q * 128:(q + 1) * 128]
                    if last:
                        E[r, at:at + 128] = e
                    acc = acc + e
            racc[r, :] = acc
            return 0
        if first:
            for a in range(NX):
                col1[0] = mb[a]
                lax.fori_loop(a * BLK // 64, (a + 1) * BLK // 64, body, 0)
        else:
            lax.fori_loop(0, ROWS // 64, body, 0)

    def row_start(t):
        to_lanes(racc, rowp.at[t], jnp.sum)
        for n, (a, b) in enumerate(xy):
            send(rowp.at[t], row_in.at[t, n], r_send.at[t], r_recv.at[t], dev(0, a, 0, b))

    def row_end(t):
        take(row_in.at[t], r_recv.at[t])
        total = rowp[t]
        for n in range(len(xy)):
            total = total + row_in[t, n]
        return 1.0 / total

    def col_pass():
        half = COLS // 2
        for h in range(2):
            def body(i, acc):
                r = rows_at(i, 64)
                rb = rbc[r, :]
                parts = []
                for q in range(half // 128):
                    p = E[r, h * half + q * 128:h * half + (q + 1) * 128] * rb
                    parts.append(acc[q] + jnp.sum(p.reshape(8, 8, 128), axis=0))
                return tuple(parts)
            acc = lax.fori_loop(
                0, ROWS // 64, body, tuple(jnp.zeros((8, 128), F32) for _ in range(half // 128))
            )
            for q in range(half // 128):
                k = h * half + q * 128
                yield k, jnp.sum(acc[q], axis=0, keepdims=True)

    def col_start(t):
        for k, v in col_pass():
            col2[t, k // CH:k // CH + 1, k % CH:k % CH + 128] = v
        for n, (a, b) in enumerate(zc):
            send(col2.at[t], col2_in.at[t, n], c_send.at[t], c_recv.at[t], dev(a, 0, b, 0))

    def col_end(t):
        take(col2_in.at[t], c_recv.at[t])
        total = col2[t]
        for n in range(len(zc)):
            total = total + col2_in[t, n]
        cvec[...] = 1.0 / total

    loads[2].wait()
    teacher_block(x)
    loads[3].wait()
    student_block(x)
    for a in (1, 3, 2):
        other = (x + a) % NX
        take(Tf.at[other], t_recv.at[other])
        teacher_block(other)

    m_loc = jnp.maximum(jnp.maximum(mb[0], mb[1]), jnp.maximum(mb[2], mb[3]))
    tot = jnp.zeros((NCH, CH), F32)
    for a in range(NX):
        tot = tot + sb[a] * jnp.exp2((mb[a] - m_loc) * T_EXP)
    col1[0] = m_loc
    col1[1] = tot
    for n, (a, b) in enumerate(zc):
        send(col1, col1_in.at[n], c1_send, c1_recv, dev(a, 0, b, 0))

    for a in (1, 3):
        other = (x + a) % NX
        take(Sf.at[other], s_recv.at[other])
        student_block(other)

    take(col1_in, c1_recv)
    for n in range(len(zc)):
        take(col1, c1_send)
    top = col1[0]
    for n in range(len(zc)):
        top = jnp.maximum(top, col1_in[n, 0])
    tot = col1[1] * jnp.exp2((col1[0] - top) * T_EXP)
    for n in range(len(zc)):
        tot = tot + col1_in[n, 1] * jnp.exp2((col1_in[n, 0] - top) * T_EXP)
    cvec[...] = 1.0 / tot
    for a in range(NX):
        mb[a] = jnp.exp2((mb[a] - top) * T_EXP)

    row_pass(True, False)
    row_start(0)
    other = (x + 2) % NX
    take(Sf.at[other], s_recv.at[other])
    student_block(other)
    to_lanes(smx, stat.at[0], jnp.max)
    to_lanes(sfac, stat.at[1], jnp.sum)
    for n, (a, b) in enumerate(xy):
        send(stat, stat_in.at[n], st_send, st_recv, dev(0, a, 0, b))
    to_rows(row_end(0), rbc)

    col_start(0)
    for a in range(NX):
        SfT[:, a * BLK:(a + 1) * BLK] = Sf[a].T

    def flip(i, _):
        k = pl.ds(pl.multiple_of(i * D, D), D)
        SpT[k, :] = Sp[:, k].T
        return 0
    lax.fori_loop(0, COLS // D, flip, 0)
    col_end(0)

    row_pass(False, False)
    row_start(1)
    take(stat_in, st_recv)
    top = stat[0]
    for n in range(len(xy)):
        top = jnp.maximum(top, stat_in[n, 0])
    tot = stat[1] * jnp.exp2((stat[0] - top) * S_EXP)
    for n in range(len(xy)):
        tot = tot + stat_in[n, 1] * jnp.exp2((stat_in[n, 0] - top) * S_EXP)
    gain = 16 * COLS / STUDENT_TEMP
    to_rows(jnp.exp2((stat[0] - top) * S_EXP) / tot * gain, gbc)

    def scale_student(i, _):
        r = rows_at(i, 64)
        g = gbc[r, :]
        for q in range(COLS // 128):
            S[r, q * 128:(q + 1) * 128] = S[r, q * 128:(q + 1) * 128] * g
        return 0
    lax.fori_loop(0, ROWS // 64, scale_student, 0)
    to_rows(row_end(1), rbc)

    col_start(1)
    col_end(1)
    row_pass(False, True)
    row_start(2)
    to_rows(row_end(2) * gain, rbc)

    def stage_g(j):
        def body(i, _):
            r = rows_at(i, 64)
            rb = rbc[r, :]
            for q in range(CH // 128):
                k = pl.ds(pl.multiple_of(j * CH + q * 128, 128), 128)
                G[r, k] = (S[r, k] - E[r, k] * rb).astype(BF16)
            return 0
        lax.fori_loop(0, ROWS // 64, body, 0)
        part = jnp.dot(SfT[...], G[:, chunk(j)], preferred_element_type=F32)
        gp[j] = part.reshape(16, NC, 8, CH)
        send(gp.at[j, :, 1 - c], gp_in.at[j], gp_send, gp_recv.at[j], dev(0, 0, 1, 0))

    def stage_c(j):
        take(gp_in.at[j], gp_recv.at[j])
        both = gp[j, :, c] + gp_in[j]
        gp_in[j] = both
        zs[j] = both.reshape(NZ, 4 * 8, CH).astype(BF16)
        for a in (1, 3, 2):
            send(zs.at[j, (z + a) % NZ], zs_in.at[j, a - 1], z_send, z_recv.at[j], dev(a, 0, 0, 0))

    def stage_z(j):
        take(zs_in.at[j], z_recv.at[j])
        total = gp_in[j, pl.ds(z * 4, 4)]
        for a in range(3):
            total = total + zs_in[j, a].astype(F32).reshape(NX, 8, CH)
        xs[j] = total * (1.0 / math.sqrt(BLK * 32))
        here = pl.ds(pl.multiple_of(x * COLS + j * CH, CH), CH)
        outp[:, here] = xs[j, x]
        for a in (1, 3, 2):
            send(xs.at[j, (x + a) % NX], outp.at[:, here], x_send, x_recv, dev(0, a, 0, 0))

    def stage_f(a):
        block = (x + a) % NX
        part = jnp.dot(G[rows_at(block, BLK), :], SpT[...], preferred_element_type=F32)
        gfs[block] = part.astype(BF16)
        if a == 0:
            gfown[...] = part
        for b in range(NY):
            if a or b:
                quarter = pl.ds(pl.multiple_of((y + b) % NY * 64, 64), 64)
                send(gfs.at[block, quarter], gfs_in.at[a * 4 + b - 1], f_send, f_recv, dev(0, a, 0, b))

    stage_g(0)
    stage_g(1)
    stage_c(0)

    def steady(j, _):
        stage_g(j)
        stage_c(j - 1)
        stage_z(j - 2)
        return 0
    lax.fori_loop(2, NCH, steady, 0)
    stage_f(2)
    stage_c(NCH - 1)
    stage_f(1)
    stage_f(3)
    stage_z(NCH - 2)
    stage_f(0)
    stage_z(NCH - 1)

    take(gfs_in, f_recv)
    own = pl.ds(pl.multiple_of(y * 64, 64), 64)
    total = gfown[own, :]
    for n in range(len(xy)):
        total = total + gfs_in[n].astype(F32)
    outf[own, :] = total * (1.0 / math.sqrt(16 * COLS))
    for b in (1, 3, 2):
        send(outf.at[own, :], outf.at[own, :], y_send, y_recv, dev(0, 0, 0, b))
    take(outp.at[:, pl.ds(0, 3 * COLS)], x_recv)
    take(outf.at[pl.ds(0, 192), :], y_recv)

    for n in range(3):
        take(Tf.at[0], t_send)
        take(Sf.at[0], s_send)
    for t in range(ITERS):
        take(row_in.at[t], r_send.at[t])
    for t in range(ITERS - 1):
        take(col2_in.at[t], c_send.at[t])
    take(stat_in, st_send)
    take(gp_in, gp_send)
    take(zs_in, z_send)
    take(outp.at[:, pl.ds(0, 3 * COLS)], x_send)
    take(gfs_in, f_send)
    take(outf.at[pl.ds(0, 192), :], y_send)


def per_device(teacher_feats, teacher_protos, student_feats, student_protos):
    V, sem = pltpu.VMEM, pltpu.SemaphoreType.DMA
    scratch = [
        V((ROWS, COLS), F32), V((ROWS, COLS), F32), V((ROWS, COLS), BF16),
        V((D, COLS), BF16), V((D, COLS), BF16), V((COLS, D), BF16),
        V((NX, BLK, D), BF16), V((NX, BLK, D), BF16), V((D, ROWS), BF16),
        V((ROWS, 128), F32), V((ROWS, 128), F32), V((ROWS, 128), F32), V((ROWS, 128), F32), V((ROWS, 128), F32),
        V((NX, NCH, CH), F32), V((NX, NCH, CH), F32), V((NCH, CH), F32),
        V((2, NCH, CH), F32), V((7, 2, NCH, CH), F32), V((2, NCH, CH), F32), V((2, 7, NCH, CH), F32),
        V((ITERS, 8, 128), F32), V((ITERS, 15, 8, 128), F32), V((2, 8, 128), F32), V((15, 2, 8, 128), F32),
        V((NCH, 16, NC, 8, CH), F32), V((NCH, 16, 8, CH), F32),
        V((NCH, NZ, 32, CH), BF16), V((NCH, 3, 32, CH), BF16), V((NCH, NX, 8, CH), F32),
        V((NX, BLK, D), BF16), V((15, 64, D), BF16), V((BLK, D), F32),
        sem((4,)), sem, sem((NX,)), sem, sem((NX,)), sem, sem, sem((2,)), sem((2,)),
        sem((ITERS,)), sem((ITERS,)), sem, sem, sem, sem((NCH,)), sem, sem((NCH,)), sem, sem,
        sem, sem, sem, sem,
    ]
    any_spec = pl.BlockSpec(memory_space=pl.ANY)
    vmem_spec = pl.BlockSpec(memory_space=pltpu.VMEM)
    return pl.pallas_call(
        kernel,
        out_shape=(
            jax.ShapeDtypeStruct((8, NX * COLS), F32),
            jax.ShapeDtypeStruct((BLK, D), F32),
        ),
        in_specs=[any_spec] * 4,
        out_specs=(vmem_spec, vmem_spec),
        scratch_shapes=scratch,
        compiler_params=pltpu.CompilerParams(
            collective_id=0, has_side_effects=True, vmem_limit_bytes=62 << 20
        ),
    )(teacher_feats, teacher_protos, student_feats, student_protos)


def solution(mesh):
    return jax.shard_map(
        per_device,
        mesh=mesh,
        in_specs=(P("dp", None), P(None, "proto"), P("dp", None), P(None, "proto")),
        out_specs=(P("dp", "proto"), P("dp", None)),
        check_vma=False,
    )
```

```python
import functools
import math

import jax
import jax.numpy as jnp
from jax import lax
from jax.experimental import pallas as pl
from jax.experimental.pallas import tpu as pltpu
from jax.sharding import PartitionSpec as P

MESH = pl.DeviceIdType.MESH
F32 = jnp.float32
BF16 = jnp.bfloat16

TEACHER_TEMP = 0.04
STUDENT_TEMP = 0.1
LOG2E = math.log2(math.e)
T_EXP = LOG2E / TEACHER_TEMP
S_EXP = LOG2E / STUDENT_TEMP

NX, NY, NZ, NC = 4, 4, 4, 2
BLK = 256
ROWS = NX * BLK
COLS = 4096
CH = 512
NCH = COLS // CH
D = 256
GP = 4
ITERS = 3


def kernel(
    tf_hbm, tp_hbm, sf_hbm, sp_hbm, outp, outf,
    E, S, G, Tp, Sp, SpT, Tf, Sf, SfT, racc, rbc, gbc, smx, sfac,
    mb, sb, cvec, col1, col1_in, col2, col2_in, rowp, row_in, stat, stat_in,
    gp, gp_in, zs, zs_in, xs, gfs, gfs_in, gfown,
    local_sem, t_send, t_recv, s_send, s_recv, c1_send, c1_recv, c_send, c_recv,
    r_send, r_recv, st_send, st_recv, gp_send, gp_recv, z_send, z_recv, x_send, x_recv,
    f_send, f_recv, y_send, y_recv,
):
    dp = lax.axis_index("dp")
    y = lax.axis_index("proto")
    z, x, c = dp // 8, (dp // 2) % 4, dp % 2

    def dev(dz, dx, dc, dy):
        zz, xx, cc, yy = (z + dz) % NZ, (x + dx) % NX, (c + dc) % NC, (y + dy) % NY
        return {"dp": zz * 8 + xx * 2 + cc, "proto": yy}

    xy = [(a, b) for a in range(NX) for b in range(NY) if (a, b) != (0, 0)]
    zc = [(a, b) for a in range(NZ) for b in range(NC) if (a, b) != (0, 0)]

    def send(src, dst, ssem, rsem, where):
        pltpu.make_async_remote_copy(
            src_ref=src, dst_ref=dst, send_sem=ssem, recv_sem=rsem, device_id=where, device_id_type=MESH
        ).start()

    def take(ref, sem):
        pltpu.make_async_copy(ref, ref, sem).wait()

    def chunk(j):
        return pl.ds(pl.multiple_of(j * CH, CH), CH)

    def rows_at(i, n):
        return pl.ds(pl.multiple_of(i * n, n), n)

    barrier = pltpu.get_barrier_semaphore()
    for a, b in xy:
        pl.semaphore_signal(barrier, inc=1, device_id=dev(0, a, 0, b), device_id_type=MESH)
    for a, b in zc:
        pl.semaphore_signal(barrier, inc=1, device_id=dev(a, 0, b, 0), device_id_type=MESH)

    mine = pl.ds(pl.multiple_of(x * COLS, COLS), COLS)
    loads = [
        pltpu.make_async_copy(tf_hbm, Tf.at[x], local_sem.at[0]),
        pltpu.make_async_copy(sf_hbm, Sf.at[rows_at(x, BLK)], local_sem.at[1]),
        pltpu.make_async_copy(tp_hbm.at[:, mine], Tp, local_sem.at[2]),
        pltpu.make_async_copy(sp_hbm.at[:, mine], Sp, local_sem.at[3]),
    ]
    for load in loads:
        load.start()
    pl.semaphore_wait(barrier, len(xy) + len(zc))
    for a in (1, 3, 2):
        send(tf_hbm, Tf.at[x], t_send, t_recv.at[x], dev(0, a, 0, 0))

    def teacher_block(a):
        block = rows_at(a, BLK)
        for j in range(NCH):
            k = slice(j * CH, (j + 1) * CH)
            s = jnp.dot(Tf[a], Tp[:, k], preferred_element_type=F32)
            m = jnp.max(s, axis=0, keepdims=True)
            e = jnp.exp2((s - m) * T_EXP)
            E[block, k] = e
            mb[a, j:j + 1, :] = m
            sb[a, j:j + 1, :] = jnp.sum(e, axis=0, keepdims=True)

    def lane_parts(v, op):
        out = v[:, :128]
        for q in range(1, v.shape[1] // 128):
            out = op(out, v[:, q * 128:(q + 1) * 128])
        return out

    def to_lanes(src, dst, op):
        for i in range(8):
            t = src[i * 128:(i + 1) * 128, :].T
            dst[i:i + 1, :] = op(t, axis=0, keepdims=True)

    def to_rows(v, dst):
        for i in range(8):
            dst[i * 128:(i + 1) * 128, :] = jnp.broadcast_to(v[i:i + 1, :], (128, 128)).T

    def student_scores():
        for j in range(NCH):
            k = slice(j * CH, (j + 1) * CH)
            s = jnp.dot(Sf[...], Sp[:, k], preferred_element_type=F32)
            S[:, k] = s
            m = lane_parts(s, jnp.maximum)
            smx[...] = m if j == 0 else jnp.maximum(smx[...], m)

    def student_exps():
        for i in range(ROWS // 128):
            r = slice(i * 128, (i + 1) * 128)
            smx[r, :] = jnp.broadcast_to(jnp.max(smx[r, :], axis=1, keepdims=True), (128, 128))

        def body(i, _):
            r = rows_at(i, 64)
            m = smx[r, :]
            acc = jnp.zeros((64, 128), F32)
            for q in range(COLS // 128):
                e = jnp.exp2((S[r, q * 128:(q + 1) * 128] - m) * S_EXP)
                S[r, q * 128:(q + 1) * 128] = e
                acc = acc + e
            sfac[r, :] = acc
            return 0
        lax.fori_loop(0, ROWS // 64, body, 0)

    def row_pass(first, last):
        def body(i, _):
            r = rows_at(i, 64)
            acc = jnp.zeros((64, 128), F32)
            for j in range(NCH):
                for q in range(CH // 128):
                    at = j * CH + q * 128
                    e = E[r, at:at + 128]
                    if first:
                        e = e * col1[j:j + 1, q * 128:(q + 1) * 128]
                        E[r, at:at + 128] = e
                    e = e * cvec[j:j + 1, q * 128:(q + 1) * 128]
                    if last:
                        E[r, at:at + 128] = e
                    acc = acc + e
            racc[r, :] = acc
            return 0
        if first:
            for a in range(NX):
                col1[...] = mb[a]
                lax.fori_loop(a * BLK // 64, (a + 1) * BLK // 64, body, 0)
        else:
            lax.fori_loop(0, ROWS // 64, body, 0)

    def row_start(t):
        to_lanes(racc, rowp.at[t], jnp.sum)
        for n, (a, b) in enumerate(xy):
            send(rowp.at[t], row_in.at[t, n], r_send.at[t], r_recv.at[t], dev(0, a, 0, b))

    def row_end(t):
        take(row_in.at[t], r_recv.at[t])
        total = rowp[t]
        for n in range(len(xy)):
            total = total + row_in[t, n]
        return 1.0 / total

    def col_pass():
        half = COLS // 2
        for h in range(2):
            def body(i, acc):
                r = rows_at(i, 64)
                rb = rbc[r, :]
                parts = []
                for q in range(half // 128):
                    p = E[r, h * half + q * 128:h * half + (q + 1) * 128] * rb
                    parts.append(acc[q] + jnp.sum(p.reshape(8, 8, 128), axis=0))
                return tuple(parts)
            acc = lax.fori_loop(
                0, ROWS // 64, body, tuple(jnp.zeros((8, 128), F32) for _ in range(half // 128))
            )
            for q in range(half // 128):
                k = h * half + q * 128
                yield k, jnp.sum(acc[q], axis=0, keepdims=True)

    def col_start(t):
        for k, v in col_pass():
            col2[t, k // CH:k // CH + 1, k % CH:k % CH + 128] = v
        for n, (a, b) in enumerate(zc):
            send(col2.at[t], col2_in.at[t, n], c_send.at[t], c_recv.at[t], dev(a, 0, b, 0))

    def col_end(t):
        take(col2_in.at[t], c_recv.at[t])
        total = col2[t]
        for n in range(len(zc)):
            total = total + col2_in[t, n]
        cvec[...] = 1.0 / total

    loads[0].wait()
    loads[2].wait()
    teacher_block(x)
    loads[1].wait()
    for a in (1, 3, 2):
        other = (x + a) % NX
        take(Tf.at[other], t_recv.at[other])
        if a == 3:
            for d in (1, 3, 2):
                send(sf_hbm, Sf.at[rows_at(x, BLK)], s_send, s_recv.at[x], dev(0, d, 0, 0))
        teacher_block(other)

    m_loc = jnp.maximum(jnp.maximum(mb[0], mb[1]), jnp.maximum(mb[2], mb[3]))
    tot = jnp.zeros((NCH, CH), F32)
    for a in range(NX):
        tot = tot + sb[a] * jnp.exp2((mb[a] - m_loc) * T_EXP)
    col1[...] = m_loc + jnp.log(tot) * TEACHER_TEMP
    for n, (a, b) in enumerate(zc):
        send(col1, col1_in.at[n], c1_send, c1_recv, dev(a, 0, b, 0))

    loads[3].wait()

    def flip(i, _):
        k = pl.ds(pl.multiple_of(i * D, D), D)
        SpT[k, :] = Sp[:, k].T
        return 0
    lax.fori_loop(0, COLS // D, flip, 0)

    take(col1_in, c1_recv)
    for n in range(len(zc)):
        take(col1, c1_send)
    top = col1[...]
    for n in range(len(zc)):
        top = jnp.maximum(top, col1_in[n])
    tot = jnp.exp2((col1[...] - top) * T_EXP)
    for n in range(len(zc)):
        tot = tot + jnp.exp2((col1_in[n] - top) * T_EXP)
    cvec[...] = 1.0 / tot
    for a in range(NX):
        mb[a] = jnp.exp2((mb[a] - top) * T_EXP)

    row_pass(True, False)
    row_start(0)
    for a in (1, 3, 2):
        other = (x + a) % NX
        take(Sf.at[rows_at(other, BLK)], s_recv.at[other])
    student_scores()
    to_rows(row_end(0), rbc)

    col_start(0)
    student_exps()
    to_lanes(smx, stat.at[0], jnp.max)
    to_lanes(sfac, stat.at[1], jnp.sum)
    for n, (a, b) in enumerate(xy):
        send(stat, stat_in.at[n], st_send, st_recv, dev(0, a, 0, b))
    col_end(0)

    row_pass(False, False)
    row_start(1)
    for a in range(NX):
        SfT[:, a * BLK:(a + 1) * BLK] = Sf[a * BLK:(a + 1) * BLK, :].T
    to_rows(row_end(1), rbc)

    col_start(1)
    take(stat_in, st_recv)
    top = stat[0]
    for n in range(len(xy)):
        top = jnp.maximum(top, stat_in[n, 0])
    tot = stat[1] * jnp.exp2((stat[0] - top) * S_EXP)
    for n in range(len(xy)):
        tot = tot + stat_in[n, 1] * jnp.exp2((stat_in[n, 0] - top) * S_EXP)
    gain = 16 * COLS / STUDENT_TEMP
    to_rows(jnp.exp2((stat[0] - top) * S_EXP) / tot * gain, gbc)

    def scale_student(i, _):
        r = rows_at(i, 64)
        g = gbc[r, :]
        for q in range(COLS // 128):
            S[r, q * 128:(q + 1) * 128] = S[r, q * 128:(q + 1) * 128] * g
        return 0
    lax.fori_loop(0, ROWS // 64, scale_student, 0)
    col_end(1)
    row_pass(False, True)
    row_start(2)
    to_rows(row_end(2) * gain, rbc)

    def logits(part):
        def body(i, _):
            r = rows_at(i, 64)
            rb = rbc[r, :]
            for q in range(part * 8, part * 8 + 8):
                k = slice(q * 128, (q + 1) * 128)
                G[r, k] = (S[r, k] - E[r, k] * rb).astype(BF16)
            return 0
        lax.fori_loop(0, ROWS // 64, body, 0)

    def stage_g(j):
        slot = j % GP
        if j >= GP:
            take(gp_in.at[slot], gp_send.at[slot])
        part = jnp.dot(SfT[...], G[:, j * CH:(j + 1) * CH], preferred_element_type=F32)
        gp[slot] = part.reshape(16, NC, 8, CH)
        send(gp.at[slot, :, 1 - c], gp_in.at[j], gp_send.at[slot], gp_recv.at[j], dev(0, 0, 1, 0))

    def stage_c(j):
        take(gp_in.at[j], gp_recv.at[j])
        both = gp[j % GP, :, c] + gp_in[j]
        gp_in[j] = both
        zs[j] = both.reshape(NZ, 4 * 8, CH).astype(BF16)
        for a in (1, 3, 2):
            send(zs.at[j, (z + a) % NZ], zs_in.at[j, a - 1], z_send, z_recv.at[j], dev(a, 0, 0, 0))

    def stage_z(j):
        take(zs_in.at[j], z_recv.at[j])
        total = gp_in[j, pl.ds(z * 4, 4)]
        for a in range(3):
            total = total + zs_in[j, a].astype(F32).reshape(NX, 8, CH)
        xs[j] = total * (1.0 / math.sqrt(BLK * 32))
        here = pl.ds(pl.multiple_of(x * COLS + j * CH, CH), CH)
        outp[:, here] = xs[j, x]
        for a in (1, 3, 2):
            send(xs.at[j, (x + a) % NX], outp.at[:, here], x_send, x_recv, dev(0, a, 0, 0))

    def stage_f(a):
        block = (x + a) % NX
        part = jnp.dot(G[rows_at(block, BLK), :], SpT[...], preferred_element_type=F32)
        gfs[block] = part.astype(BF16)
        if a == 0:
            gfown[...] = part
        for b in range(NY):
            if a or b:
                quarter = pl.ds(pl.multiple_of((y + b) % NY * 64, 64), 64)
                send(gfs.at[block, quarter], gfs_in.at[a * 4 + b - 1], f_send, f_recv, dev(0, a, 0, b))

    for part in range(NCH // 2):
        logits(part)
        for j in (2 * part, 2 * part + 1):
            stage_g(j)
            if j >= 2:
                stage_c(j - 2)
    stage_c(NCH - 2)
    stage_f(2)
    stage_c(NCH - 1)
    stage_z(0)
    stage_f(1)
    stage_z(1)
    stage_f(3)
    stage_f(0)
    for j in range(2, 5):
        stage_z(j)

    take(gfs_in, f_recv)
    own = pl.ds(pl.multiple_of(y * 64, 64), 64)
    total = gfown[own, :]
    for n in range(len(xy)):
        total = total + gfs_in[n].astype(F32)
    outf[own, :] = total * (1.0 / math.sqrt(16 * COLS))
    for b in (1, 3, 2):
        send(outf.at[own, :], outf.at[own, :], y_send, y_recv, dev(0, 0, 0, b))
    for j in range(5, NCH):
        stage_z(j)
    take(outp.at[:, pl.ds(0, 3 * COLS)], x_recv)
    take(outf.at[pl.ds(0, 192), :], y_recv)

    for n in range(3):
        take(Tf.at[0], t_send)
        take(Sf.at[rows_at(0, BLK)], s_send)
    for t in range(ITERS):
        take(row_in.at[t], r_send.at[t])
    for t in range(ITERS - 1):
        take(col2_in.at[t], c_send.at[t])
    take(stat_in, st_send)
    for slot in range(GP):
        take(gp_in.at[slot], gp_send.at[slot])
    take(zs_in, z_send)
    take(outp.at[:, pl.ds(0, 3 * COLS)], x_send)
    take(gfs_in, f_send)
    take(outf.at[pl.ds(0, 192), :], y_send)


def deliver(outp, outf, outp_hbm, outf_hbm, sems):
    copies = [
        pltpu.make_async_copy(outp, outp_hbm, sems.at[0]),
        pltpu.make_async_copy(outf, outf_hbm, sems.at[1]),
    ]
    for copy in copies:
        copy.start()
    for copy in copies:
        copy.wait()


def per_device(teacher_feats, teacher_protos, student_feats, student_protos):
    V, sem = pltpu.VMEM, pltpu.SemaphoreType.DMA
    scratch = [
        V((ROWS, COLS), F32), V((ROWS, COLS), F32), V((ROWS, COLS), BF16),
        V((D, COLS), BF16), V((D, COLS), BF16), V((COLS, D), BF16),
        V((NX, BLK, D), BF16), V((ROWS, D), BF16), V((D, ROWS), BF16),
        V((ROWS, 128), F32), V((ROWS, 128), F32), V((ROWS, 128), F32), V((ROWS, 128), F32), V((ROWS, 128), F32),
        V((NX, NCH, CH), F32), V((NX, NCH, CH), F32), V((NCH, CH), F32),
        V((NCH, CH), F32), V((7, NCH, CH), F32), V((2, NCH, CH), F32), V((2, 7, NCH, CH), F32),
        V((ITERS, 8, 128), F32), V((ITERS, 15, 8, 128), F32), V((2, 8, 128), F32), V((15, 2, 8, 128), F32),
        V((GP, 16, NC, 8, CH), F32), V((NCH, 16, 8, CH), F32),
        V((NCH, NZ, 32, CH), BF16), V((NCH, 3, 32, CH), BF16), V((NCH, NX, 8, CH), F32),
        V((NX, BLK, D), BF16), V((15, 64, D), BF16), V((BLK, D), F32),
        sem((4,)), sem, sem((NX,)), sem, sem((NX,)), sem, sem, sem((2,)), sem((2,)),
        sem((ITERS,)), sem((ITERS,)), sem, sem, sem((GP,)), sem((NCH,)), sem, sem((NCH,)), sem, sem,
        sem, sem, sem, sem,
    ]
    any_spec = pl.BlockSpec(memory_space=pl.ANY)
    vmem_spec = pl.BlockSpec(memory_space=pltpu.VMEM)
    held = pl.pallas_call(
        kernel,
        out_shape=(
            pltpu.VMEM((8, NX * COLS), F32),
            pltpu.VMEM((BLK, D), F32),
        ),
        in_specs=[any_spec] * 4,
        out_specs=(vmem_spec, vmem_spec),
        scratch_shapes=scratch,
        compiler_params=pltpu.CompilerParams(
            collective_id=0, has_side_effects=True, vmem_limit_bytes=62 << 20
        ),
    )(teacher_feats, teacher_protos, student_feats, student_protos)
    return pl.pallas_call(
        deliver,
        out_shape=(
            jax.ShapeDtypeStruct((8, NX * COLS), F32),
            jax.ShapeDtypeStruct((BLK, D), F32),
        ),
        in_specs=[vmem_spec] * 2,
        out_specs=(any_spec, any_spec),
        scratch_shapes=[sem((2,))],
    )(*(pltpu.with_memory_space_constraint(part, pltpu.VMEM) for part in held))


def solution(mesh):
    return jax.shard_map(
        per_device,
        mesh=mesh,
        in_specs=(P("dp", None), P(None, "proto"), P("dp", None), P(None, "proto")),
        out_specs=(P("dp", "proto"), P("dp", None)),
        check_vma=False,
    )
```

```python
import functools
import math

import jax
import jax.numpy as jnp
from jax import lax
from jax.experimental import pallas as pl
from jax.experimental.pallas import tpu as pltpu
from jax.sharding import PartitionSpec as P

MESH = pl.DeviceIdType.MESH
F32 = jnp.float32
BF16 = jnp.bfloat16

TEACHER_TEMP = 0.04
STUDENT_TEMP = 0.1
LOG2E = math.log2(math.e)
T_EXP = LOG2E / TEACHER_TEMP
S_EXP = LOG2E / STUDENT_TEMP

NX, NY, NZ, NC = 4, 4, 4, 2
BLK = 256
ROWS = NX * BLK
COLS = 4096
CH = 512
NCH = COLS // CH
D = 256
HALF, PIECE = BLK // 2, BLK // 2 // NY
GP = 4
ITERS = 3


def kernel(
    tf_hbm, tp_hbm, sf_hbm, sp_hbm, outp, outf,
    E, S, G, Tp, Sp, SpT, Tf, Sf, SfT, racc, rbc, gbc, smx, sfac,
    mb, sb, cvec, col1, col1_in, col2, col2_in, rowp, row_in, stat, stat_in,
    gp, gp_in, zs, zs_in, xs, gfs, gfs_in, gfown,
    local_sem, t_send, t_recv, s_send, s_recv, c1_send, c1_recv, c_send, c_recv,
    r_send, r_recv, st_send, st_recv, gp_send, gp_recv, z_send, z_recv, x_send, x_recv,
    f_send, f_recv, y_send, y_recv,
):
    dp = lax.axis_index("dp")
    y = lax.axis_index("proto")
    z, x, c = dp // 8, (dp // 2) % 4, dp % 2

    def dev(dz, dx, dc, dy):
        zz, xx, cc, yy = (z + dz) % NZ, (x + dx) % NX, (c + dc) % NC, (y + dy) % NY
        return {"dp": zz * 8 + xx * 2 + cc, "proto": yy}

    xy = [(a, b) for a in range(NX) for b in range(NY) if (a, b) != (0, 0)]
    zc = [(a, b) for a in range(NZ) for b in range(NC) if (a, b) != (0, 0)]

    far = sorted(xy, key=lambda p: -min(p[0], NX - p[0]) - min(p[1], NY - p[1]))

    def send(src, dst, ssem, rsem, where):
        pltpu.make_async_remote_copy(
            src_ref=src, dst_ref=dst, send_sem=ssem, recv_sem=rsem, device_id=where, device_id_type=MESH
        ).start()

    def take(ref, sem):
        pltpu.make_async_copy(ref, ref, sem).wait()

    def chunk(j):
        return pl.ds(pl.multiple_of(j * CH, CH), CH)

    def rows_at(i, n):
        return pl.ds(pl.multiple_of(i * n, n), n)

    barrier = pltpu.get_barrier_semaphore()
    lines = [(0, 2, 0, 0), (0, 0, 0, 2), (0, 1, 0, 0), (0, 3, 0, 0), (0, 0, 0, 1), (0, 0, 0, 3)]
    lines = [(a, 0, b, 0) for a, b in reversed(zc)] + lines
    for where in lines:
        pl.semaphore_signal(barrier, inc=1, device_id=dev(*where), device_id_type=MESH)

    mine = pl.ds(pl.multiple_of(x * COLS, COLS), COLS)
    loads = [
        pltpu.make_async_copy(tf_hbm, Tf.at[x], local_sem.at[0]),
        pltpu.make_async_copy(sf_hbm, Sf.at[rows_at(x, BLK)], local_sem.at[1]),
        pltpu.make_async_copy(tp_hbm.at[:, mine], Tp, local_sem.at[2]),
        pltpu.make_async_copy(sp_hbm.at[:, mine], Sp, local_sem.at[3]),
    ]
    for load in loads:
        load.start()
    pl.semaphore_wait(barrier, len(lines))
    for a in (1, 3, 2):
        send(tf_hbm, Tf.at[x], t_send, t_recv.at[x], dev(0, a, 0, 0))

    def teacher_block(a):
        block = rows_at(a, BLK)
        for j in range(NCH):
            k = slice(j * CH, (j + 1) * CH)
            s = jnp.dot(Tf[a], Tp[:, k], preferred_element_type=F32)
            m = jnp.max(s, axis=0, keepdims=True)
            e = jnp.exp2((s - m) * T_EXP)
            E[block, k] = e
            mb[a, j:j + 1, :] = m
            sb[a, j:j + 1, :] = jnp.sum(e, axis=0, keepdims=True)

    def lane_parts(v, op):
        out = v[:, :128]
        for q in range(1, v.shape[1] // 128):
            out = op(out, v[:, q * 128:(q + 1) * 128])
        return out

    def to_lanes(src, dst, op):
        for i in range(8):
            t = src[i * 128:(i + 1) * 128, :].T
            dst[i:i + 1, :] = op(t, axis=0, keepdims=True)

    def to_rows(v, dst):
        for i in range(8):
            dst[i * 128:(i + 1) * 128, :] = jnp.broadcast_to(v[i:i + 1, :], (128, 128)).T

    def student_scores():
        for j in range(NCH):
            k = slice(j * CH, (j + 1) * CH)
            s = jnp.dot(Sf[...], Sp[:, k], preferred_element_type=F32)
            S[:, k] = s
            m = lane_parts(s, jnp.maximum)
            smx[...] = m if j == 0 else jnp.maximum(smx[...], m)

    def student_exps():
        for i in range(ROWS // 128):
            r = slice(i * 128, (i + 1) * 128)
            smx[r, :] = jnp.broadcast_to(jnp.max(smx[r, :], axis=1, keepdims=True), (128, 128))

        def body(i, _):
            r = rows_at(i, 64)
            m = smx[r, :]
            acc = jnp.zeros((64, 128), F32)
            for q in range(COLS // 128):
                e = jnp.exp2((S[r, q * 128:(q + 1) * 128] - m) * S_EXP)
                S[r, q * 128:(q + 1) * 128] = e
                acc = acc + e
            sfac[r, :] = acc
            return 0
        lax.fori_loop(0, ROWS // 64, body, 0)

    def row_pass(first, last):
        def body(i, _):
            r = rows_at(i, 64)
            acc = jnp.zeros((64, 128), F32)
            for j in range(NCH):
                for q in range(CH // 128):
                    at = j * CH + q * 128
                    e = E[r, at:at + 128]
                    if first:
                        e = e * col1[j:j + 1, q * 128:(q + 1) * 128]
                        E[r, at:at + 128] = e
                    e = e * cvec[j:j + 1, q * 128:(q + 1) * 128]
                    if last:
                        E[r, at:at + 128] = e
                    acc = acc + e
            racc[r, :] = acc
            return 0
        if first:
            for a in range(NX):
                col1[...] = mb[a]
                lax.fori_loop(a * BLK // 64, (a + 1) * BLK // 64, body, 0)
        else:
            lax.fori_loop(0, ROWS // 64, body, 0)

    def row_start(t):
        to_lanes(racc, rowp.at[t], jnp.sum)
        for n, (a, b) in enumerate(xy):
            send(rowp.at[t], row_in.at[t, n], r_send.at[t], r_recv.at[t], dev(0, a, 0, b))

    def row_end(t):
        take(row_in.at[t], r_recv.at[t])
        total = rowp[t]
        for n in range(len(xy)):
            total = total + row_in[t, n]
        return 1.0 / total

    def col_pass():
        half = COLS // 2
        for h in range(2):
            def body(i, acc):
                r = rows_at(i, 64)
                rb = rbc[r, :]
                parts = []
                for q in range(half // 128):
                    p = E[r, h * half + q * 128:h * half + (q + 1) * 128] * rb
                    parts.append(acc[q] + jnp.sum(p.reshape(8, 8, 128), axis=0))
                return tuple(parts)
            acc = lax.fori_loop(
                0, ROWS // 64, body, tuple(jnp.zeros((8, 128), F32) for _ in range(half // 128))
            )
            for q in range(half // 128):
                k = h * half + q * 128
                yield k, jnp.sum(acc[q], axis=0, keepdims=True)

    def col_start(t):
        for k, v in col_pass():
            col2[t, k // CH:k // CH + 1, k % CH:k % CH + 128] = v
        for n, (a, b) in enumerate(zc):
            send(col2.at[t], col2_in.at[t, n], c_send.at[t], c_recv.at[t], dev(a, 0, b, 0))

    def col_end(t):
        take(col2_in.at[t], c_recv.at[t])
        total = col2[t]
        for n in range(len(zc)):
            total = total + col2_in[t, n]
        cvec[...] = 1.0 / total

    loads[0].wait()
    loads[2].wait()
    teacher_block(x)
    loads[1].wait()
    for a in (1, 3, 2):
        other = (x + a) % NX
        take(Tf.at[other], t_recv.at[other])
        if a == 3:
            for d in (1, 3, 2):
                send(sf_hbm, Sf.at[rows_at(x, BLK)], s_send, s_recv.at[x], dev(0, d, 0, 0))
        teacher_block(other)

    m_loc = jnp.maximum(jnp.maximum(mb[0], mb[1]), jnp.maximum(mb[2], mb[3]))
    tot = jnp.zeros((NCH, CH), F32)
    for a in range(NX):
        tot = tot + sb[a] * jnp.exp2((mb[a] - m_loc) * T_EXP)
    col1[...] = m_loc + jnp.log(tot) * TEACHER_TEMP
    for n, (a, b) in enumerate(zc):
        send(col1, col1_in.at[n], c1_send, c1_recv, dev(a, 0, b, 0))

    take(col1_in, c1_recv)
    for n in range(len(zc)):
        take(col1, c1_send)
    top = col1[...]
    for n in range(len(zc)):
        top = jnp.maximum(top, col1_in[n])
    tot = jnp.exp2((col1[...] - top) * T_EXP)
    for n in range(len(zc)):
        tot = tot + jnp.exp2((col1_in[n] - top) * T_EXP)
    cvec[...] = 1.0 / tot
    for a in range(NX):
        mb[a] = jnp.exp2((mb[a] - top) * T_EXP)

    row_pass(True, False)
    row_start(0)
    for a in (1, 3, 2):
        other = (x + a) % NX
        take(Sf.at[rows_at(other, BLK)], s_recv.at[other])
    loads[3].wait()
    student_scores()
    to_rows(row_end(0), rbc)

    col_start(0)
    student_exps()
    to_lanes(smx, stat.at[0], jnp.max)
    to_lanes(sfac, stat.at[1], jnp.sum)
    for n, (a, b) in enumerate(xy):
        send(stat, stat_in.at[n], st_send, st_recv, dev(0, a, 0, b))
    col_end(0)

    row_pass(False, False)
    row_start(1)
    def flip(i, _):
        k = pl.ds(pl.multiple_of(i * D, D), D)
        SpT[k, :] = Sp[:, k].T
        return 0
    lax.fori_loop(0, COLS // D, flip, 0)
    for a in range(NX):
        SfT[:, a * BLK:(a + 1) * BLK] = Sf[a * BLK:(a + 1) * BLK, :].T
    to_rows(row_end(1), rbc)

    col_start(1)
    take(stat_in, st_recv)
    top = stat[0]
    for n in range(len(xy)):
        top = jnp.maximum(top, stat_in[n, 0])
    tot = stat[1] * jnp.exp2((stat[0] - top) * S_EXP)
    for n in range(len(xy)):
        tot = tot + stat_in[n, 1] * jnp.exp2((stat_in[n, 0] - top) * S_EXP)
    gain = 16 * COLS / STUDENT_TEMP
    to_rows(jnp.exp2((stat[0] - top) * S_EXP) / tot * gain, gbc)

    def scale_student(i, _):
        r = rows_at(i, 64)
        g = gbc[r, :]
        for q in range(COLS // 128):
            S[r, q * 128:(q + 1) * 128] = S[r, q * 128:(q + 1) * 128] * g
        return 0
    lax.fori_loop(0, ROWS // 64, scale_student, 0)
    col_end(1)
    row_pass(False, True)
    row_start(2)
    to_rows(row_end(2) * gain, rbc)

    def logits(part):
        def body(i, _):
            r = rows_at(i, 64)
            rb = rbc[r, :]
            for q in range(part * 8, part * 8 + 8):
                k = slice(q * 128, (q + 1) * 128)
                G[r, k] = (S[r, k] - E[r, k] * rb).astype(BF16)
            return 0
        lax.fori_loop(0, ROWS // 64, body, 0)

    def stage_g(j):
        slot = j % GP
        if j >= GP:
            take(gp_in.at[slot], gp_send.at[slot])
        part = jnp.dot(SfT[...], G[:, j * CH:(j + 1) * CH], preferred_element_type=F32)
        gp[slot] = part.reshape(16, NC, 8, CH)
        send(gp.at[slot, :, 1 - c], gp_in.at[j], gp_send.at[slot], gp_recv.at[j], dev(0, 0, 1, 0))

    def stage_c(j):
        take(gp_in.at[j], gp_recv.at[j])
        both = gp[j % GP, :, c] + gp_in[j]
        gp_in[j] = both
        zs[j] = both.reshape(NZ, 4 * 8, CH).astype(BF16)
        for a in (1, 3, 2):
            send(zs.at[j, (z + a) % NZ], zs_in.at[j, a - 1], z_send, z_recv.at[j], dev(a, 0, 0, 0))

    def stage_z(j):
        take(zs_in.at[j], z_recv.at[j])
        total = gp_in[j, pl.ds(z * 4, 4)]
        for a in range(3):
            total = total + zs_in[j, a].astype(F32).reshape(NX, 8, CH)
        xs[j] = total * (1.0 / math.sqrt(BLK * 32))
        here = pl.ds(pl.multiple_of(x * COLS + j * CH, CH), CH)
        outp[:, here] = xs[j, x]
        for a in (1, 3, 2):
            send(xs.at[j, (x + a) % NX], outp.at[:, here], x_send, x_recv, dev(0, a, 0, 0))

    def stage_f(h):
        rows = [G[b * BLK + h * HALF:b * BLK + (h + 1) * HALF, :] for b in range(NX)]
        part = jnp.dot(jnp.concatenate(rows, axis=0), SpT[...], preferred_element_type=F32)
        part = part.reshape(NX, HALF, D)
        gfown[h] = part
        gfs[h] = part.astype(BF16)
        for n, (a, b) in enumerate(far):
            piece = pl.ds(pl.multiple_of((y + b) % NY * PIECE, PIECE), PIECE)
            send(gfs.at[h, (x + a) % NX, piece], gfs_in.at[h, n], f_send, f_recv.at[h], dev(0, a, 0, b))

    def final_f(h):
        take(gfs_in.at[h], f_recv.at[h])
        total = gfown[h, x, pl.ds(pl.multiple_of(y * PIECE, PIECE), PIECE)]
        for n in range(len(xy)):
            total = total + gfs_in[h, n].astype(F32)
        own = pl.ds(pl.multiple_of(h * HALF + y * PIECE, PIECE), PIECE)
        outf[own, :] = total * (1.0 / math.sqrt(16 * COLS))
        for b in (2, 1, 3):
            send(outf.at[own, :], outf.at[own, :], y_send, y_recv, dev(0, 0, 0, b))

    logits(0)
    stage_g(0)
    stage_g(1)
    stage_c(0)
    logits(1)
    stage_g(2)
    stage_c(1)
    logits(2)
    stage_g(3)
    stage_c(2)
    logits(3)
    stage_f(0)
    stage_z(0)
    stage_c(3)
    stage_g(4)
    stage_g(5)
    stage_z(1)
    stage_c(4)
    stage_f(1)
    stage_z(2)
    stage_c(5)
    stage_g(6)
    stage_g(7)
    stage_z(3)
    stage_c(6)
    final_f(0)
    stage_z(4)
    stage_c(7)
    stage_z(5)
    final_f(1)
    stage_z(6)
    stage_z(7)
    take(outp.at[:, pl.ds(0, 3 * COLS)], x_recv)
    take(outf.at[pl.ds(0, 192), :], y_recv)

    for n in range(3):
        take(Tf.at[0], t_send)
        take(Sf.at[rows_at(0, BLK)], s_send)
    for t in range(ITERS):
        take(row_in.at[t], r_send.at[t])
    for t in range(ITERS - 1):
        take(col2_in.at[t], c_send.at[t])
    take(stat_in, st_send)
    for slot in range(GP):
        take(gp_in.at[slot], gp_send.at[slot])
    take(zs_in, z_send)
    take(outp.at[:, pl.ds(0, 3 * COLS)], x_send)
    take(gfs_in, f_send)
    take(outf.at[pl.ds(0, 192), :], y_send)


def deliver(outp, outf, outp_hbm, outf_hbm, sems):
    copies = [
        pltpu.make_async_copy(outp, outp_hbm, sems.at[0]),
        pltpu.make_async_copy(outf, outf_hbm, sems.at[1]),
    ]
    for copy in copies:
        copy.start()
    for copy in copies:
        copy.wait()


def per_device(teacher_feats, teacher_protos, student_feats, student_protos):
    V, sem = pltpu.VMEM, pltpu.SemaphoreType.DMA
    scratch = [
        V((ROWS, COLS), F32), V((ROWS, COLS), F32), V((ROWS, COLS), BF16),
        V((D, COLS), BF16), V((D, COLS), BF16), V((COLS, D), BF16),
        V((NX, BLK, D), BF16), V((ROWS, D), BF16), V((D, ROWS), BF16),
        V((ROWS, 128), F32), V((ROWS, 128), F32), V((ROWS, 128), F32), V((ROWS, 128), F32), V((ROWS, 128), F32),
        V((NX, NCH, CH), F32), V((NX, NCH, CH), F32), V((NCH, CH), F32),
        V((NCH, CH), F32), V((7, NCH, CH), F32), V((2, NCH, CH), F32), V((2, 7, NCH, CH), F32),
        V((ITERS, 8, 128), F32), V((ITERS, 15, 8, 128), F32), V((2, 8, 128), F32), V((15, 2, 8, 128), F32),
        V((GP, 16, NC, 8, CH), F32), V((NCH, 16, 8, CH), F32),
        V((NCH, NZ, 32, CH), BF16), V((NCH, 3, 32, CH), BF16), V((NCH, NX, 8, CH), F32),
        V((2, NX, HALF, D), BF16), V((2, 15, PIECE, D), BF16), V((2, NX, HALF, D), F32),
        sem((4,)), sem, sem((NX,)), sem, sem((NX,)), sem, sem, sem((2,)), sem((2,)),
        sem((ITERS,)), sem((ITERS,)), sem, sem, sem((GP,)), sem((NCH,)), sem, sem((NCH,)), sem, sem,
        sem, sem((2,)), sem, sem,
    ]
    any_spec = pl.BlockSpec(memory_space=pl.ANY)
    vmem_spec = pl.BlockSpec(memory_space=pltpu.VMEM)
    held = pl.pallas_call(
        kernel,
        out_shape=(
            pltpu.VMEM((8, NX * COLS), F32),
            pltpu.VMEM((BLK, D), F32),
        ),
        in_specs=[any_spec] * 4,
        out_specs=(vmem_spec, vmem_spec),
        scratch_shapes=scratch,
        compiler_params=pltpu.CompilerParams(
            collective_id=0, has_side_effects=True, vmem_limit_bytes=62 << 20
        ),
    )(teacher_feats, teacher_protos, student_feats, student_protos)
    return pl.pallas_call(
        deliver,
        out_shape=(
            jax.ShapeDtypeStruct((8, NX * COLS), F32),
            jax.ShapeDtypeStruct((BLK, D), F32),
        ),
        in_specs=[vmem_spec] * 2,
        out_specs=(any_spec, any_spec),
        scratch_shapes=[sem((2,))],
    )(*(pltpu.with_memory_space_constraint(part, pltpu.VMEM) for part in held))


def solution(mesh):
    return jax.shard_map(
        per_device,
        mesh=mesh,
        in_specs=(P("dp", None), P(None, "proto"), P("dp", None), P(None, "proto")),
        out_specs=(P("dp", "proto"), P("dp", None)),
        check_vma=False,
    )
```

```python
import functools
import math

import jax
import jax.numpy as jnp
from jax import lax
from jax.experimental import pallas as pl
from jax.experimental.pallas import tpu as pltpu
from jax.sharding import PartitionSpec as P

MESH = pl.DeviceIdType.MESH
F32 = jnp.float32
BF16 = jnp.bfloat16

TEACHER_TEMP = 0.04
STUDENT_TEMP = 0.1
LOG2E = math.log2(math.e)
T_EXP = LOG2E / TEACHER_TEMP
S_EXP = LOG2E / STUDENT_TEMP

NX, NY, NZ, NC = 4, 4, 4, 2
BLK = 256
ROWS = NX * BLK
COLS = 4096
CH = 512
NCH = COLS // CH
D = 256
HALF, PIECE = BLK // 2, BLK // 2 // NY
GP = 4
ITERS = 3


def kernel(
    tf_hbm, tp_hbm, sf_hbm, sp_hbm, outp, outf,
    E, S, G, Tp, Sp, SpT, Tf, Sf, SfT, racc, rbc, gbc, smx, sfac,
    mb, sb, cvec, col1, col1_in, col2, col2_in, rowp, row_in, stat, stat_in,
    gp, gown, gp_in, zown, zs, zs_in, xs, gfs, gfs_in, gfown,
    local_sem, t_send, t_recv, s_send, s_recv, c1_send, c1_recv, c_send, c_recv,
    r_send, r_recv, st_send, st_recv, gp_send, gp_recv, z_send, z_recv, x_send, x_recv,
    f_send, f_recv, y_send, y_recv,
):
    dp = lax.axis_index("dp")
    y = lax.axis_index("proto")
    z, x, c = dp // 8, (dp // 2) % 4, dp % 2

    def dev(dz, dx, dc, dy):
        zz, xx, cc, yy = (z + dz) % NZ, (x + dx) % NX, (c + dc) % NC, (y + dy) % NY
        return {"dp": zz * 8 + xx * 2 + cc, "proto": yy}

    def hops(p):
        return -min(p[0], 4 - p[0]) - min(p[1], 4 - p[1])

    xy = sorted([(a, b) for a in range(NX) for b in range(NY) if (a, b) != (0, 0)], key=hops)
    zc = sorted([(a, b) for a in range(NZ) for b in range(NC) if (a, b) != (0, 0)], key=hops)

    def send(src, dst, ssem, rsem, where):
        pltpu.make_async_remote_copy(
            src_ref=src, dst_ref=dst, send_sem=ssem, recv_sem=rsem, device_id=where, device_id_type=MESH
        ).start()

    def take(ref, sem):
        pltpu.make_async_copy(ref, ref, sem).wait()

    def chunk(j):
        return pl.ds(pl.multiple_of(j * CH, CH), CH)

    def rows_at(i, n):
        return pl.ds(pl.multiple_of(i * n, n), n)

    barrier = pltpu.get_barrier_semaphore()
    lines = [(0, 2, 0, 0), (0, 0, 0, 2), (0, 1, 0, 0), (0, 3, 0, 0), (0, 0, 0, 1), (0, 0, 0, 3)]
    lines = [(a, 0, b, 0) for a, b in zc] + lines
    for where in lines:
        pl.semaphore_signal(barrier, inc=1, device_id=dev(*where), device_id_type=MESH)

    mine = pl.ds(pl.multiple_of(x * COLS, COLS), COLS)
    loads = [
        pltpu.make_async_copy(tf_hbm, Tf.at[x], local_sem.at[0]),
        pltpu.make_async_copy(sf_hbm, Sf.at[rows_at(x, BLK)], local_sem.at[1]),
        pltpu.make_async_copy(tp_hbm.at[:, mine], Tp, local_sem.at[2]),
        pltpu.make_async_copy(sp_hbm.at[:, mine], Sp, local_sem.at[3]),
    ]
    for load in loads:
        load.start()
    pl.semaphore_wait(barrier, len(lines))
    for a in (1, 3, 2):
        send(tf_hbm, Tf.at[x], t_send, t_recv.at[x], dev(0, a, 0, 0))

    def teacher_block(a):
        block = rows_at(a, BLK)
        for j in range(NCH):
            k = slice(j * CH, (j + 1) * CH)
            s = jnp.dot(Tf[a], Tp[:, k], preferred_element_type=F32)
            m = jnp.max(s, axis=0, keepdims=True)
            e = jnp.exp2((s - m) * T_EXP)
            E[block, k] = e
            mb[a, j:j + 1, :] = m
            sb[a, j:j + 1, :] = jnp.sum(e, axis=0, keepdims=True)

    def lane_parts(v, op):
        out = v[:, :128]
        for q in range(1, v.shape[1] // 128):
            out = op(out, v[:, q * 128:(q + 1) * 128])
        return out

    def to_lanes(src, dst, op):
        for i in range(8):
            t = src[i * 128:(i + 1) * 128, :].T
            dst[i:i + 1, :] = op(t, axis=0, keepdims=True)

    def to_rows(v, dst):
        for i in range(8):
            dst[i * 128:(i + 1) * 128, :] = jnp.broadcast_to(v[i:i + 1, :], (128, 128)).T

    def student_scores():
        for j in range(NCH):
            k = slice(j * CH, (j + 1) * CH)
            s = jnp.dot(Sf[...], Sp[:, k], preferred_element_type=F32)
            S[:, k] = s
            m = lane_parts(s, jnp.maximum)
            smx[...] = m if j == 0 else jnp.maximum(smx[...], m)

    def student_exps(lo, hi):
        for i in range(lo, hi):
            r = slice(i * 128, (i + 1) * 128)
            smx[r, :] = jnp.broadcast_to(jnp.max(smx[r, :], axis=1, keepdims=True), (128, 128))

        def body(i, _):
            r = rows_at(i, 64)
            m = smx[r, :]
            acc = jnp.zeros((64, 128), F32)
            for q in range(COLS // 128):
                e = jnp.exp2((S[r, q * 128:(q + 1) * 128] - m) * S_EXP)
                S[r, q * 128:(q + 1) * 128] = e
                acc = acc + e
            sfac[r, :] = acc
            return 0
        lax.fori_loop(lo * 2, hi * 2, body, 0)

    def row_pass(first, last):
        def body(i, _):
            r = rows_at(i, 64)
            acc = jnp.zeros((64, 128), F32)
            for j in range(NCH):
                for q in range(CH // 128):
                    at = j * CH + q * 128
                    e = E[r, at:at + 128]
                    if first:
                        e = e * col1[j:j + 1, q * 128:(q + 1) * 128]
                        E[r, at:at + 128] = e
                    e = e * cvec[j:j + 1, q * 128:(q + 1) * 128]
                    if last:
                        E[r, at:at + 128] = e
                    acc = acc + e
            racc[r, :] = acc
            return 0
        if first:
            for a in range(NX):
                col1[...] = mb[a]
                lax.fori_loop(a * BLK // 64, (a + 1) * BLK // 64, body, 0)
        else:
            lax.fori_loop(0, ROWS // 64, body, 0)

    def row_start(t):
        to_lanes(racc, rowp.at[t], jnp.sum)
        for n, (a, b) in enumerate(xy):
            send(rowp.at[t], row_in.at[t, n], r_send.at[t], r_recv.at[t], dev(0, a, 0, b))

    def row_end(t):
        take(row_in.at[t], r_recv.at[t])
        total = rowp[t]
        for n in range(len(xy)):
            total = total + row_in[t, n]
        return 1.0 / total

    def col_pass():
        half = COLS // 2
        for h in range(2):
            def body(i, acc):
                r = rows_at(i, 64)
                rb = rbc[r, :]
                parts = []
                for q in range(half // 128):
                    p = E[r, h * half + q * 128:h * half + (q + 1) * 128] * rb
                    parts.append(acc[q] + jnp.sum(p.reshape(8, 8, 128), axis=0))
                return tuple(parts)
            acc = lax.fori_loop(
                0, ROWS // 64, body, tuple(jnp.zeros((8, 128), F32) for _ in range(half // 128))
            )
            for q in range(half // 128):
                k = h * half + q * 128
                yield k, jnp.sum(acc[q], axis=0, keepdims=True)

    def col_start(t):
        for k, v in col_pass():
            col2[t, k // CH:k // CH + 1, k % CH:k % CH + 128] = v
        for n, (a, b) in enumerate(zc):
            send(col2.at[t], col2_in.at[t, n], c_send.at[t], c_recv.at[t], dev(a, 0, b, 0))

    def col_end(t):
        take(col2_in.at[t], c_recv.at[t])
        total = col2[t]
        for n in range(len(zc)):
            total = total + col2_in[t, n]
        cvec[...] = 1.0 / total

    loads[0].wait()
    loads[2].wait()
    teacher_block(x)
    loads[1].wait()
    for a in (1, 3, 2):
        other = (x + a) % NX
        take(Tf.at[other], t_recv.at[other])
        if a == 3:
            for d in (1, 3, 2):
                send(sf_hbm, Sf.at[rows_at(x, BLK)], s_send, s_recv.at[x], dev(0, d, 0, 0))
        teacher_block(other)

    m_loc = jnp.maximum(jnp.maximum(mb[0], mb[1]), jnp.maximum(mb[2], mb[3]))
    tot = jnp.zeros((NCH, CH), F32)
    for a in range(NX):
        tot = tot + sb[a] * jnp.exp2((mb[a] - m_loc) * T_EXP)
    col1[...] = m_loc + jnp.log(tot) * TEACHER_TEMP
    for n, (a, b) in enumerate(zc):
        send(col1, col1_in.at[n], c1_send, c1_recv, dev(a, 0, b, 0))

    take(col1_in, c1_recv)
    for n in range(len(zc)):
        take(col1, c1_send)
    top = col1[...]
    for n in range(len(zc)):
        top = jnp.maximum(top, col1_in[n])
    tot = jnp.exp2((col1[...] - top) * T_EXP)
    for n in range(len(zc)):
        tot = tot + jnp.exp2((col1_in[n] - top) * T_EXP)
    cvec[...] = 1.0 / tot
    for a in range(NX):
        mb[a] = jnp.exp2((mb[a] - top) * T_EXP)

    row_pass(True, False)
    row_start(0)
    for a in (1, 3, 2):
        other = (x + a) % NX
        take(Sf.at[rows_at(other, BLK)], s_recv.at[other])
    loads[3].wait()
    student_scores()
    student_exps(0, 4)
    to_rows(row_end(0), rbc)

    col_start(0)
    student_exps(4, 8)
    to_lanes(smx, stat.at[0], jnp.max)
    to_lanes(sfac, stat.at[1], jnp.sum)
    for n, (a, b) in enumerate(xy):
        send(stat, stat_in.at[n], st_send, st_recv, dev(0, a, 0, b))
    col_end(0)

    row_pass(False, False)
    row_start(1)
    def flip(i, _):
        k = pl.ds(pl.multiple_of(i * D, D), D)
        SpT[k, :] = Sp[:, k].T
        return 0
    lax.fori_loop(0, COLS // D, flip, 0)
    for a in range(NX):
        SfT[:, a * BLK:(a + 1) * BLK] = Sf[a * BLK:(a + 1) * BLK, :].T
    to_rows(row_end(1), rbc)

    col_start(1)
    take(stat_in, st_recv)
    top = stat[0]
    for n in range(len(xy)):
        top = jnp.maximum(top, stat_in[n, 0])
    tot = stat[1] * jnp.exp2((stat[0] - top) * S_EXP)
    for n in range(len(xy)):
        tot = tot + stat_in[n, 1] * jnp.exp2((stat_in[n, 0] - top) * S_EXP)
    gain = 16 * COLS / STUDENT_TEMP
    to_rows(jnp.exp2((stat[0] - top) * S_EXP) / tot * gain, gbc)

    def scale_student(i, _):
        r = rows_at(i, 64)
        g = gbc[r, :]
        for q in range(COLS // 128):
            S[r, q * 128:(q + 1) * 128] = S[r, q * 128:(q + 1) * 128] * g
        return 0
    lax.fori_loop(0, ROWS // 64, scale_student, 0)
    col_end(1)
    row_pass(False, True)
    row_start(2)
    to_rows(row_end(2) * gain, rbc)

    def logits(part):
        def body(i, _):
            r = rows_at(i, 64)
            rb = rbc[r, :]
            for q in range(part * 8, part * 8 + 8):
                k = slice(q * 128, (q + 1) * 128)
                G[r, k] = (S[r, k] - E[r, k] * rb).astype(BF16)
            return 0
        lax.fori_loop(0, ROWS // 64, body, 0)

    def stage_g(j):
        slot = j % GP
        if j >= GP:
            take(gp_in.at[slot], gp_send.at[slot])
        part = jnp.dot(SfT[...], G[:, j * CH:(j + 1) * CH], preferred_element_type=F32)
        part = part.reshape(16, NC, 8, CH)
        for h in range(NC):
            half = part[:, h].reshape(D // NC, CH)
            gown[slot, h] = half
            gp[slot, h] = half.astype(BF16)
        send(gp.at[slot, 1 - c], gp_in.at[j], gp_send.at[slot], gp_recv.at[j], dev(0, 0, 1, 0))

    def stage_c(j):
        take(gp_in.at[j], gp_recv.at[j])
        both = (gown[j % GP, c] + gp_in[j].astype(F32)).reshape(NZ, 4 * 8, CH)
        zown[j] = both
        zs[j] = both.astype(BF16)
        for a in (1, 3, 2):
            send(zs.at[j, (z + a) % NZ], zs_in.at[j, a - 1], z_send, z_recv.at[j], dev(a, 0, 0, 0))

    def stage_z(j):
        take(zs_in.at[j], z_recv.at[j])
        total = zown[j, z].reshape(NX, 8, CH)
        for a in range(3):
            total = total + zs_in[j, a].astype(F32).reshape(NX, 8, CH)
        xs[j] = total * (1.0 / math.sqrt(BLK * 32))
        here = pl.ds(pl.multiple_of(x * COLS + j * CH, CH), CH)
        outp[:, here] = xs[j, x]
        for a in (1, 3, 2):
            send(xs.at[j, (x + a) % NX], outp.at[:, here], x_send, x_recv, dev(0, a, 0, 0))

    def stage_f(h):
        rows = [G[b * BLK + h * HALF:b * BLK + (h + 1) * HALF, :] for b in range(NX)]
        part = jnp.dot(jnp.concatenate(rows, axis=0), SpT[...], preferred_element_type=F32)
        part = part.reshape(NX, HALF, D)
        gfown[h] = part
        gfs[h] = part.astype(BF16)
        for n, (a, b) in enumerate(xy):
            piece = pl.ds(pl.multiple_of((y + b) % NY * PIECE, PIECE), PIECE)
            send(gfs.at[h, (x + a) % NX, piece], gfs_in.at[h, n], f_send, f_recv.at[h], dev(0, a, 0, b))

    def final_f(h):
        take(gfs_in.at[h], f_recv.at[h])
        total = gfown[h, x, pl.ds(pl.multiple_of(y * PIECE, PIECE), PIECE)]
        for n in range(len(xy)):
            total = total + gfs_in[h, n].astype(F32)
        own = pl.ds(pl.multiple_of(h * HALF + y * PIECE, PIECE), PIECE)
        outf[own, :] = total * (1.0 / math.sqrt(16 * COLS))
        for b in (2, 1, 3):
            send(outf.at[own, :], outf.at[own, :], y_send, y_recv, dev(0, 0, 0, b))

    logits(0)
    stage_g(0)
    stage_g(1)
    logits(1)
    stage_c(0)
    stage_g(2)
    stage_c(1)
    logits(2)
    stage_g(3)
    stage_c(2)
    logits(3)
    stage_g(4)
    stage_c(3)
    stage_f(0)
    stage_z(0)
    stage_g(5)
    stage_c(4)
    stage_f(1)
    stage_z(1)
    stage_c(5)
    stage_g(6)
    stage_g(7)
    stage_z(2)
    stage_c(6)
    stage_z(3)
    stage_c(7)
    stage_z(4)
    final_f(0)
    stage_z(5)
    stage_z(6)
    final_f(1)
    stage_z(7)
    take(outp.at[:, pl.ds(0, 3 * COLS)], x_recv)
    take(outf.at[pl.ds(0, 192), :], y_recv)

    for n in range(3):
        take(Tf.at[0], t_send)
        take(Sf.at[rows_at(0, BLK)], s_send)
    for t in range(ITERS):
        take(row_in.at[t], r_send.at[t])
    for t in range(ITERS - 1):
        take(col2_in.at[t], c_send.at[t])
    take(stat_in, st_send)
    for slot in range(GP):
        take(gp_in.at[slot], gp_send.at[slot])
    take(zs_in, z_send)
    take(outp.at[:, pl.ds(0, 3 * COLS)], x_send)
    take(gfs_in, f_send)
    take(outf.at[pl.ds(0, 192), :], y_send)


def deliver(outp, outf, outp_hbm, outf_hbm, sems):
    copies = [
        pltpu.make_async_copy(outp, outp_hbm, sems.at[0]),
        pltpu.make_async_copy(outf, outf_hbm, sems.at[1]),
    ]
    for copy in copies:
        copy.start()
    for copy in copies:
        copy.wait()


def per_device(teacher_feats, teacher_protos, student_feats, student_protos):
    V, sem = pltpu.VMEM, pltpu.SemaphoreType.DMA
    scratch = [
        V((ROWS, COLS), F32), V((ROWS, COLS), F32), V((ROWS, COLS), BF16),
        V((D, COLS), BF16), V((D, COLS), BF16), V((COLS, D), BF16),
        V((NX, BLK, D), BF16), V((ROWS, D), BF16), V((D, ROWS), BF16),
        V((ROWS, 128), F32), V((ROWS, 128), F32), V((ROWS, 128), F32), V((ROWS, 128), F32), V((ROWS, 128), F32),
        V((NX, NCH, CH), F32), V((NX, NCH, CH), F32), V((NCH, CH), F32),
        V((NCH, CH), F32), V((7, NCH, CH), F32), V((2, NCH, CH), F32), V((2, 7, NCH, CH), F32),
        V((ITERS, 8, 128), F32), V((ITERS, 15, 8, 128), F32), V((2, 8, 128), F32), V((15, 2, 8, 128), F32),
        V((GP, NC, D // NC, CH), BF16), V((GP, NC, D // NC, CH), F32), V((NCH, D // NC, CH), BF16),
        V((NCH, NZ, 32, CH), F32),
        V((NCH, NZ, 32, CH), BF16), V((NCH, 3, 32, CH), BF16), V((NCH, NX, 8, CH), F32),
        V((2, NX, HALF, D), BF16), V((2, 15, PIECE, D), BF16), V((2, NX, HALF, D), F32),
        sem((4,)), sem, sem((NX,)), sem, sem((NX,)), sem, sem, sem((2,)), sem((2,)),
        sem((ITERS,)), sem((ITERS,)), sem, sem, sem((GP,)), sem((NCH,)), sem, sem((NCH,)), sem, sem,
        sem, sem((2,)), sem, sem,
    ]
    any_spec = pl.BlockSpec(memory_space=pl.ANY)
    vmem_spec = pl.BlockSpec(memory_space=pltpu.VMEM)
    held = pl.pallas_call(
        kernel,
        out_shape=(
            pltpu.VMEM((8, NX * COLS), F32),
            pltpu.VMEM((BLK, D), F32),
        ),
        in_specs=[any_spec] * 4,
        out_specs=(vmem_spec, vmem_spec),
        scratch_shapes=scratch,
        compiler_params=pltpu.CompilerParams(
            collective_id=0, has_side_effects=True, vmem_limit_bytes=62 << 20
        ),
    )(teacher_feats, teacher_protos, student_feats, student_protos)
    return pl.pallas_call(
        deliver,
        out_shape=(
            jax.ShapeDtypeStruct((8, NX * COLS), F32),
            jax.ShapeDtypeStruct((BLK, D), F32),
        ),
        in_specs=[vmem_spec] * 2,
        out_specs=(any_spec, any_spec),
        scratch_shapes=[sem((2,))],
    )(*(pltpu.with_memory_space_constraint(part, pltpu.VMEM) for part in held))


def solution(mesh):
    return jax.shard_map(
        per_device,
        mesh=mesh,
        in_specs=(P("dp", None), P(None, "proto"), P("dp", None), P(None, "proto")),
        out_specs=(P("dp", "proto"), P("dp", None)),
        check_vma=False,
    )
```

```python
import functools
import math

import jax
import jax.numpy as jnp
from jax import lax
from jax.experimental import pallas as pl
from jax.experimental.pallas import tpu as pltpu
from jax.sharding import PartitionSpec as P

MESH = pl.DeviceIdType.MESH
F32 = jnp.float32
BF16 = jnp.bfloat16

TEACHER_TEMP = 0.04
STUDENT_TEMP = 0.1
LOG2E = math.log2(math.e)
T_EXP = LOG2E / TEACHER_TEMP
S_EXP = LOG2E / STUDENT_TEMP

NX, NY, NZ, NC = 4, 4, 4, 2
BLK = 256
ROWS = NX * BLK
COLS = 4096
CH = 512
NCH = COLS // CH
D = 256
HALF, PIECE = BLK // 2, BLK // 2 // NY
GP = 4
ITERS = 3


def kernel(
    tf_hbm, tp_hbm, sf_hbm, sp_hbm, outp, outf,
    E, S, G, Tp, Sp, SpT, Tf, Sf, SfT, racc, rbc, gbc, smx, sfac,
    mb, sb, cvec, col1, col1_in, col2, col2_in, rowp, row_in, stat, stat_in,
    gp, gown, gp_in, zown, zs, zs_in, xs, gfs, gfs_in, gfown,
    local_sem, t_send, t_recv, s_send, s_recv, c1_send, c1_recv, c_send, c_recv,
    r_send, r_recv, st_send, st_recv, gp_send, gp_recv, z_send, z_recv, x_send, x_recv,
    f_send, f_recv, y_send, y_recv,
):
    dp = lax.axis_index("dp")
    y = lax.axis_index("proto")
    z, x, c = dp // 8, (dp // 2) % 4, dp % 2

    def dev(dz, dx, dc, dy):
        zz, xx, cc, yy = (z + dz) % NZ, (x + dx) % NX, (c + dc) % NC, (y + dy) % NY
        return {"dp": zz * 8 + xx * 2 + cc, "proto": yy}

    def hops(p):
        return -min(p[0], 4 - p[0]) - min(p[1], 4 - p[1])

    xy = sorted([(a, b) for a in range(NX) for b in range(NY) if (a, b) != (0, 0)], key=hops)
    zc = sorted([(a, b) for a in range(NZ) for b in range(NC) if (a, b) != (0, 0)], key=hops)

    def send(src, dst, ssem, rsem, where):
        pltpu.make_async_remote_copy(
            src_ref=src, dst_ref=dst, send_sem=ssem, recv_sem=rsem, device_id=where, device_id_type=MESH
        ).start()

    def take(ref, sem):
        pltpu.make_async_copy(ref, ref, sem).wait()

    def chunk(j):
        return pl.ds(pl.multiple_of(j * CH, CH), CH)

    def rows_at(i, n):
        return pl.ds(pl.multiple_of(i * n, n), n)

    barrier = pltpu.get_barrier_semaphore()
    lines = [(0, 2, 0, 0), (0, 0, 0, 2), (0, 1, 0, 0), (0, 3, 0, 0), (0, 0, 0, 1), (0, 0, 0, 3)]
    lines = [(a, 0, b, 0) for a, b in zc] + lines
    for where in lines:
        pl.semaphore_signal(barrier, inc=1, device_id=dev(*where), device_id_type=MESH)

    mine = pl.ds(pl.multiple_of(x * COLS, COLS), COLS)
    loads = [
        pltpu.make_async_copy(tf_hbm, Tf.at[x], local_sem.at[0]),
        pltpu.make_async_copy(sf_hbm, Sf.at[rows_at(x, BLK)], local_sem.at[1]),
        pltpu.make_async_copy(tp_hbm.at[:, mine], Tp, local_sem.at[2]),
        pltpu.make_async_copy(sp_hbm.at[:, mine], Sp, local_sem.at[3]),
    ]
    loads[0].start()
    loads[2].start()
    pl.semaphore_wait(barrier, len(lines))
    for a in (1, 3, 2):
        send(tf_hbm, Tf.at[x], t_send, t_recv.at[x], dev(0, a, 0, 0))

    def teacher_block(a):
        block = rows_at(a, BLK)
        for j in range(NCH):
            k = slice(j * CH, (j + 1) * CH)
            s = jnp.dot(Tf[a], Tp[:, k], preferred_element_type=F32)
            m = jnp.max(s, axis=0, keepdims=True)
            e = jnp.exp2((s - m) * T_EXP)
            E[block, k] = e
            mb[a, j:j + 1, :] = m
            sb[a, j:j + 1, :] = jnp.sum(e, axis=0, keepdims=True)

    def lane_parts(v, op):
        out = v[:, :128]
        for q in range(1, v.shape[1] // 128):
            out = op(out, v[:, q * 128:(q + 1) * 128])
        return out

    def to_lanes(src, dst, op):
        for i in range(8):
            t = src[i * 128:(i + 1) * 128, :].T
            dst[i:i + 1, :] = op(t, axis=0, keepdims=True)

    def to_rows(v, dst):
        for i in range(8):
            dst[i * 128:(i + 1) * 128, :] = jnp.broadcast_to(v[i:i + 1, :], (128, 128)).T

    def student_scores():
        for j in range(NCH):
            k = slice(j * CH, (j + 1) * CH)
            s = jnp.dot(Sf[...], Sp[:, k], preferred_element_type=F32)
            S[:, k] = s
            m = lane_parts(s, jnp.maximum)
            smx[...] = m if j == 0 else jnp.maximum(smx[...], m)

    def student_exps(lo, hi):
        for i in range(lo, hi):
            r = slice(i * 128, (i + 1) * 128)
            smx[r, :] = jnp.broadcast_to(jnp.max(smx[r, :], axis=1, keepdims=True), (128, 128))

        def body(i, _):
            r = rows_at(i, 64)
            m = smx[r, :]
            acc = jnp.zeros((64, 128), F32)
            for q in range(COLS // 128):
                e = jnp.exp2((S[r, q * 128:(q + 1) * 128] - m) * S_EXP)
                S[r, q * 128:(q + 1) * 128] = e
                acc = acc + e
            sfac[r, :] = acc
            return 0
        lax.fori_loop(lo * 2, hi * 2, body, 0)

    def row_pass(first, last):
        def body(i, _):
            r = rows_at(i, 64)
            acc = jnp.zeros((64, 128), F32)
            for j in range(NCH):
                for q in range(CH // 128):
                    at = j * CH + q * 128
                    e = E[r, at:at + 128]
                    if first:
                        e = e * col1[j:j + 1, q * 128:(q + 1) * 128]
                        E[r, at:at + 128] = e
                    e = e * cvec[j:j + 1, q * 128:(q + 1) * 128]
                    if last:
                        E[r, at:at + 128] = e
                    acc = acc + e
            racc[r, :] = acc
            return 0
        if first:
            for a in range(NX):
                col1[...] = mb[a]
                lax.fori_loop(a * BLK // 64, (a + 1) * BLK // 64, body, 0)
        else:
            lax.fori_loop(0, ROWS // 64, body, 0)

    def row_start(t):
        to_lanes(racc, rowp.at[t], jnp.sum)
        for n, (a, b) in enumerate(xy):
            send(rowp.at[t], row_in.at[t, n], r_send.at[t], r_recv.at[t], dev(0, a, 0, b))

    def row_end(t):
        take(row_in.at[t], r_recv.at[t])
        total = rowp[t]
        for n in range(len(xy)):
            total = total + row_in[t, n]
        return 1.0 / total

    def col_pass():
        half = COLS // 2
        for h in range(2):
            def body(i, acc):
                r = rows_at(i, 64)
                rb = rbc[r, :]
                parts = []
                for q in range(half // 128):
                    p = E[r, h * half + q * 128:h * half + (q + 1) * 128] * rb
                    parts.append(acc[q] + jnp.sum(p.reshape(8, 8, 128), axis=0))
                return tuple(parts)
            acc = lax.fori_loop(
                0, ROWS // 64, body, tuple(jnp.zeros((8, 128), F32) for _ in range(half // 128))
            )
            for q in range(half // 128):
                k = h * half + q * 128
                yield k, jnp.sum(acc[q], axis=0, keepdims=True)

    def col_start(t):
        for k, v in col_pass():
            col2[t, k // CH:k // CH + 1, k % CH:k % CH + 128] = v
        for n, (a, b) in enumerate(zc):
            send(col2.at[t], col2_in.at[t, n], c_send.at[t], c_recv.at[t], dev(a, 0, b, 0))

    def col_end(t):
        take(col2_in.at[t], c_recv.at[t])
        total = col2[t]
        for n in range(len(zc)):
            total = total + col2_in[t, n]
        cvec[...] = 1.0 / total

    loads[0].wait()
    loads[2].wait()
    teacher_block(x)
    loads[1].start()
    loads[3].start()
    for a in (1, 3, 2):
        other = (x + a) % NX
        take(Tf.at[other], t_recv.at[other])
        if a == 3:
            for d in (1, 3, 2):
                send(sf_hbm, Sf.at[rows_at(x, BLK)], s_send, s_recv.at[x], dev(0, d, 0, 0))
        teacher_block(other)

    m_loc = jnp.maximum(jnp.maximum(mb[0], mb[1]), jnp.maximum(mb[2], mb[3]))
    tot = jnp.zeros((NCH, CH), F32)
    for a in range(NX):
        tot = tot + sb[a] * jnp.exp2((mb[a] - m_loc) * T_EXP)
    col1[...] = m_loc + jnp.log(tot) * TEACHER_TEMP
    for n, (a, b) in enumerate(zc):
        send(col1, col1_in.at[n], c1_send, c1_recv, dev(a, 0, b, 0))

    take(col1_in, c1_recv)
    for n in range(len(zc)):
        take(col1, c1_send)
    top = col1[...]
    for n in range(len(zc)):
        top = jnp.maximum(top, col1_in[n])
    tot = jnp.exp2((col1[...] - top) * T_EXP)
    for n in range(len(zc)):
        tot = tot + jnp.exp2((col1_in[n] - top) * T_EXP)
    cvec[...] = 1.0 / tot
    for a in range(NX):
        mb[a] = jnp.exp2((mb[a] - top) * T_EXP)

    row_pass(True, False)
    row_start(0)
    for a in (1, 3, 2):
        other = (x + a) % NX
        take(Sf.at[rows_at(other, BLK)], s_recv.at[other])
    loads[1].wait()
    loads[3].wait()
    student_scores()
    student_exps(0, 4)
    to_rows(row_end(0), rbc)

    col_start(0)
    student_exps(4, 8)
    to_lanes(smx, stat.at[0], jnp.max)
    to_lanes(sfac, stat.at[1], jnp.sum)
    for n, (a, b) in enumerate(xy):
        send(stat, stat_in.at[n], st_send, st_recv, dev(0, a, 0, b))
    col_end(0)

    row_pass(False, False)
    row_start(1)
    def flip(i, _):
        k = pl.ds(pl.multiple_of(i * D, D), D)
        SpT[k, :] = Sp[:, k].T
        return 0
    lax.fori_loop(0, COLS // D, flip, 0)
    for a in range(NX):
        SfT[:, a * BLK:(a + 1) * BLK] = Sf[a * BLK:(a + 1) * BLK, :].T
    to_rows(row_end(1), rbc)

    col_start(1)
    take(stat_in, st_recv)
    top = stat[0]
    for n in range(len(xy)):
        top = jnp.maximum(top, stat_in[n, 0])
    tot = stat[1] * jnp.exp2((stat[0] - top) * S_EXP)
    for n in range(len(xy)):
        tot = tot + stat_in[n, 1] * jnp.exp2((stat_in[n, 0] - top) * S_EXP)
    gain = 16 * COLS / STUDENT_TEMP
    to_rows(jnp.exp2((stat[0] - top) * S_EXP) / tot * gain, gbc)

    def scale_student(i, _):
        r = rows_at(i, 64)
        g = gbc[r, :]
        for q in range(COLS // 128):
            S[r, q * 128:(q + 1) * 128] = S[r, q * 128:(q + 1) * 128] * g
        return 0
    lax.fori_loop(0, ROWS // 64, scale_student, 0)
    col_end(1)
    row_pass(False, True)
    row_start(2)
    to_rows(row_end(2) * gain, rbc)

    def logits(part):
        def body(i, _):
            r = rows_at(i, 64)
            rb = rbc[r, :]
            for q in range(part * 8, part * 8 + 8):
                k = slice(q * 128, (q + 1) * 128)
                G[r, k] = (S[r, k] - E[r, k] * rb).astype(BF16)
            return 0
        lax.fori_loop(0, ROWS // 64, body, 0)

    def stage_g(j):
        slot = j % GP
        if j >= GP:
            take(gp_in.at[slot], gp_send.at[slot])
        part = jnp.dot(SfT[...], G[:, j * CH:(j + 1) * CH], preferred_element_type=F32)
        part = part.reshape(16, NC, 8, CH)
        for h in range(NC):
            half = part[:, h].reshape(D // NC, CH)
            gown[slot, h] = half
            gp[slot, h] = half.astype(BF16)
        send(gp.at[slot, 1 - c], gp_in.at[j], gp_send.at[slot], gp_recv.at[j], dev(0, 0, 1, 0))

    def stage_c(j):
        take(gp_in.at[j], gp_recv.at[j])
        both = (gown[j % GP, c] + gp_in[j].astype(F32)).reshape(NZ, 4 * 8, CH)
        zown[j] = both
        zs[j] = both.astype(BF16)
        for a in (1, 3, 2):
            send(zs.at[j, (z + a) % NZ], zs_in.at[j, a - 1], z_send, z_recv.at[j], dev(a, 0, 0, 0))

    def stage_z(j):
        take(zs_in.at[j], z_recv.at[j])
        total = zown[j, z].reshape(NX, 8, CH)
        for a in range(3):
            total = total + zs_in[j, a].astype(F32).reshape(NX, 8, CH)
        xs[j] = total * (1.0 / math.sqrt(BLK * 32))
        here = pl.ds(pl.multiple_of(x * COLS + j * CH, CH), CH)
        outp[:, here] = xs[j, x]
        for a in (1, 3, 2):
            send(xs.at[j, (x + a) % NX], outp.at[:, here], x_send, x_recv, dev(0, a, 0, 0))

    def stage_f(h):
        rows = [G[b * BLK + h * HALF:b * BLK + (h + 1) * HALF, :] for b in range(NX)]
        part = jnp.dot(jnp.concatenate(rows, axis=0), SpT[...], preferred_element_type=F32)
        part = part.reshape(NX, HALF, D)
        gfown[h] = part
        gfs[h] = part.astype(BF16)
        for n, (a, b) in enumerate(xy):
            piece = pl.ds(pl.multiple_of((y + b) % NY * PIECE, PIECE), PIECE)
            send(gfs.at[h, (x + a) % NX, piece], gfs_in.at[h, n], f_send, f_recv.at[h], dev(0, a, 0, b))

    def final_f(h):
        take(gfs_in.at[h], f_recv.at[h])
        total = gfown[h, x, pl.ds(pl.multiple_of(y * PIECE, PIECE), PIECE)]
        for n in range(len(xy)):
            total = total + gfs_in[h, n].astype(F32)
        own = pl.ds(pl.multiple_of(h * HALF + y * PIECE, PIECE), PIECE)
        outf[own, :] = total * (1.0 / math.sqrt(16 * COLS))
        for b in (2, 1, 3):
            send(outf.at[own, :], outf.at[own, :], y_send, y_recv, dev(0, 0, 0, b))

    logits(0)
    stage_g(0)
    logits(1)
    stage_g(1)
    stage_c(0)
    stage_g(2)
    logits(2)
    stage_c(1)
    stage_g(3)
    logits(3)
    stage_c(2)
    stage_g(4)
    stage_c(3)
    stage_f(0)
    stage_g(5)
    stage_z(0)
    stage_c(4)
    stage_f(1)
    stage_z(1)
    stage_c(5)
    stage_g(6)
    stage_g(7)
    stage_z(2)
    stage_z(3)
    stage_c(6)
    stage_c(7)
    stage_z(4)
    final_f(0)
    stage_z(5)
    stage_z(6)
    final_f(1)
    stage_z(7)
    take(outp.at[:, pl.ds(0, 3 * COLS)], x_recv)
    take(outf.at[pl.ds(0, 192), :], y_recv)

    for n in range(3):
        take(Tf.at[0], t_send)
        take(Sf.at[rows_at(0, BLK)], s_send)
    for t in range(ITERS):
        take(row_in.at[t], r_send.at[t])
    for t in range(ITERS - 1):
        take(col2_in.at[t], c_send.at[t])
    take(stat_in, st_send)
    for slot in range(GP):
        take(gp_in.at[slot], gp_send.at[slot])
    take(zs_in, z_send)
    take(outp.at[:, pl.ds(0, 3 * COLS)], x_send)
    take(gfs_in, f_send)
    take(outf.at[pl.ds(0, 192), :], y_send)


def deliver(outp, outf, outp_hbm, outf_hbm, sems):
    copies = [
        pltpu.make_async_copy(outp, outp_hbm, sems.at[0]),
        pltpu.make_async_copy(outf, outf_hbm, sems.at[1]),
    ]
    for copy in copies:
        copy.start()
    for copy in copies:
        copy.wait()


def per_device(teacher_feats, teacher_protos, student_feats, student_protos):
    V, sem = pltpu.VMEM, pltpu.SemaphoreType.DMA
    scratch = [
        V((ROWS, COLS), F32), V((ROWS, COLS), F32), V((ROWS, COLS), BF16),
        V((D, COLS), BF16), V((D, COLS), BF16), V((COLS, D), BF16),
        V((NX, BLK, D), BF16), V((ROWS, D), BF16), V((D, ROWS), BF16),
        V((ROWS, 128), F32), V((ROWS, 128), F32), V((ROWS, 128), F32), V((ROWS, 128), F32), V((ROWS, 128), F32),
        V((NX, NCH, CH), F32), V((NX, NCH, CH), F32), V((NCH, CH), F32),
        V((NCH, CH), F32), V((7, NCH, CH), F32), V((2, NCH, CH), F32), V((2, 7, NCH, CH), F32),
        V((ITERS, 8, 128), F32), V((ITERS, 15, 8, 128), F32), V((2, 8, 128), F32), V((15, 2, 8, 128), F32),
        V((GP, NC, D // NC, CH), BF16), V((GP, NC, D // NC, CH), F32), V((NCH, D // NC, CH), BF16),
        V((NCH, NZ, 32, CH), F32),
        V((NCH, NZ, 32, CH), BF16), V((NCH, 3, 32, CH), BF16), V((NCH, NX, 8, CH), F32),
        V((2, NX, HALF, D), BF16), V((2, 15, PIECE, D), BF16), V((2, NX, HALF, D), F32),
        sem((4,)), sem, sem((NX,)), sem, sem((NX,)), sem, sem, sem((2,)), sem((2,)),
        sem((ITERS,)), sem((ITERS,)), sem, sem, sem((GP,)), sem((NCH,)), sem, sem((NCH,)), sem, sem,
        sem, sem((2,)), sem, sem,
    ]
    any_spec = pl.BlockSpec(memory_space=pl.ANY)
    vmem_spec = pl.BlockSpec(memory_space=pltpu.VMEM)
    held = pl.pallas_call(
        kernel,
        out_shape=(
            pltpu.VMEM((8, NX * COLS), F32),
            pltpu.VMEM((BLK, D), F32),
        ),
        in_specs=[any_spec] * 4,
        out_specs=(vmem_spec, vmem_spec),
        scratch_shapes=scratch,
        compiler_params=pltpu.CompilerParams(
            collective_id=0, has_side_effects=True, vmem_limit_bytes=62 << 20
        ),
    )(teacher_feats, teacher_protos, student_feats, student_protos)
    return pl.pallas_call(
        deliver,
        out_shape=(
            jax.ShapeDtypeStruct((8, NX * COLS), F32),
            jax.ShapeDtypeStruct((BLK, D), F32),
        ),
        in_specs=[vmem_spec] * 2,
        out_specs=(any_spec, any_spec),
        scratch_shapes=[sem((2,))],
    )(*(pltpu.with_memory_space_constraint(part, pltpu.VMEM) for part in held))


def solution(mesh):
    return jax.shard_map(
        per_device,
        mesh=mesh,
        in_specs=(P("dp", None), P(None, "proto"), P("dp", None), P(None, "proto")),
        out_specs=(P("dp", "proto"), P("dp", None)),
        check_vma=False,
    )
```
